512 devices in a mesh: section: 32 (over z, x_hi), dp: 16 (over y, x_lo, core).
Axes of the slice: x: 4 (x_hi: 2, x_lo: 2; x = x_hi * 2 + x_lo), y: 4, z: 16, core: 2. Of those that a mesh axis runs over, the one named last changes fastest.
Arguments:
- acts: bfloat16 [32, 2048, 5120], P('section', 'dp'), may hold values from -6 to 6
- scores: float32 [32, 32, 64, 64], P('section', 'dp'), may hold values from -10 to 400
- segments: int32 [32, 64], P('dp'), may hold values from 0 to 63, as said below
- cotangent: bfloat16 [2048, 5120], P('dp'), may hold values from -6 to 6
- w_value: bfloat16 [32, 5120, 128], P('section', 'dp'), may hold values from -0.078125 to 0.078125
- w_out: bfloat16 [32, 5120, 128], P('section', 'dp'), may hold values from -0.25 to 0.25
Outputs:
- grad_input: bfloat16 [32, 2048, 5120], P('section', 'dp')
- grad_value: float32 [32, 5120, 128], P('section', 'dp')
- grad_out: float32 [32, 5120, 128], P('section', 'dp')
The draws below stay inside these ranges and needn't reach their ends.
Inputs may be any that keep to these rules, and one draw needn't show every extreme that they name: `segments`: document ids start at 0 in each sequence, never fall along it and rise by at most one from a token to the next.
All inputs are finite; a program needn't handle non-finite values.
Results may differ from the reference program's by a relative error of at most 0.04.
Values may be sent and summed in bfloat16 or wider, within the bound.
A program may use at most 64 MiB of HBM per device.

```python
import jax
import jax.numpy as jnp
from jax import lax

D = 5120
HEAD_WIDTH = 128
SEQUENCE_TOKENS = 64
SECTIONS = 32
TOK_DEV = 128
TOKENS = 2048
SEQUENCE_COUNT = 32
N_DP = 16


def segment_ids(key):
    key = jax.random.fold_in(key, 11)
    new_flags = jax.random.randint(key, (SEQUENCE_COUNT, SEQUENCE_TOKENS), 0, 4) == 0
    places = jnp.arange(SEQUENCE_TOKENS)
    sequence_rows = jnp.arange(SEQUENCE_COUNT)
    new_flags = jnp.where((places[None, :] == 0) | (sequence_rows[:, None] == 0), True, new_flags)
    return jnp.cumsum(new_flags.astype(jnp.int32), axis=1) - 1


def draw_segments(key, part):
    return segment_ids(key)


def draw_scores(key, part):
    key = jax.random.fold_in(key, 5)
    key_base = jax.random.fold_in(key, 0)
    shape = (SECTIONS, SEQUENCE_COUNT, SEQUENCE_TOKENS, SEQUENCE_TOKENS)
    raw_scores = jnp.clip(jax.random.normal(key_base, shape, jnp.float32) * 2.0, -10.0, 10.0)
    return raw_scores


def steps_of(own_key, dims, cuts, low, high):
    gain, own = 1.0, jax.random.fold_in(own_key, 6)
    for position, blocks in cuts:
        draws = jnp.exp(jax.random.uniform(jax.random.fold_in(own, position), (blocks,), jnp.float32, low / len(cuts), high / len(cuts)))
        gain = gain * jnp.repeat(draws, dims[position] // blocks).reshape([-1 if axis == position else 1 for axis in range(len(dims))])
    return gain


def normal_values(key, extent, width, most, cuts=(), held_as=jnp.bfloat16):
    loudness = steps_of(key, extent, cuts, -0.22, 0.18) if cuts else 1.0
    values = jax.random.normal(key, extent, jnp.float32) * width * loudness
    return jnp.minimum(jnp.maximum(values, -most), most).astype(held_as)


def setup_inputs(seed: int = 0) -> dict:
    arg_keys = jax.random.split(jax.random.key(seed), 7)
    acts = normal_values(arg_keys[0], (SECTIONS, TOKENS, D), 1.0, 6.0, ((0, 32), (1, 16)))
    scores = draw_scores(jax.random.fold_in(arg_keys[6], 71), 0)
    segments = draw_segments(jax.random.fold_in(arg_keys[6], 71), 0)
    cotangent = normal_values(arg_keys[3], (TOKENS, D), 1.0, 6.0, ((0, 16),))
    w_value = normal_values(arg_keys[4], (SECTIONS, D, HEAD_WIDTH), D ** -0.5, 0.078125, ((0, 32), (1, 16)))
    w_out = normal_values(arg_keys[5], (SECTIONS, D, HEAD_WIDTH), (4 * HEAD_WIDTH) ** -0.5, 0.25, ((0, 32), (1, 16)))
    return {"acts": acts, "scores": scores, "segments": segments, "cotangent": cotangent, "w_value": w_value, "w_out": w_out}


def masked_probs(logits, doc_ids):
    places = jnp.arange(SEQUENCE_TOKENS)
    allowed = (places[None, :, None] >= places[None, None, :]) & (doc_ids[:, :, None] == doc_ids[:, None, :])
    kept = jnp.where(allowed, logits, -jnp.inf)
    row_top = jnp.max(kept, axis=-1, keepdims=True)
    expo = jnp.where(allowed, jnp.exp(kept - row_top), jnp.zeros_like(logits))
    return (expo / jnp.sum(expo, axis=-1, keepdims=True)).astype(jnp.bfloat16)


def reference(acts, scores, segments, cotangent, w_value, w_out):
    incoming = cotangent
    input_list = []
    value_list = []
    out_list = []
    for layer_index in reversed(range(SECTIONS)):
        tokens = acts[layer_index]
        probs = masked_probs(scores[layer_index], segments)
        probability_full = probs.astype(jnp.float32)
        projected_output = jnp.dot(tokens, w_value[layer_index], preferred_element_type=jnp.float32).astype(jnp.bfloat16)
        mixed_values = jnp.einsum("xzj,xjs->xzs", probability_full, projected_output.reshape(SEQUENCE_COUNT, SEQUENCE_TOKENS, HEAD_WIDTH).astype(jnp.float32)).astype(jnp.bfloat16)
        mixed_values = mixed_values.reshape(TOKENS, HEAD_WIDTH)
        head_gradient = jnp.dot(incoming, w_out[layer_index], preferred_element_type=jnp.float32).astype(jnp.bfloat16)
        value_gradient = jnp.einsum("ztj,ztf->zjf", probability_full, head_gradient.reshape(SEQUENCE_COUNT, SEQUENCE_TOKENS, HEAD_WIDTH).astype(jnp.float32)).astype(jnp.bfloat16)
        value_gradient = value_gradient.reshape(TOKENS, HEAD_WIDTH)
        spread = lax.dot_general(value_gradient, w_value[layer_index], (((1,), (1,)), ((), ())), preferred_element_type=jnp.float32)
        result = (incoming.astype(jnp.float32) + spread).astype(jnp.bfloat16)
        blocks = jnp.einsum("rtd,rth->rdh", incoming.reshape(N_DP, TOK_DEV, D).astype(jnp.float32), mixed_values.reshape(N_DP, TOK_DEV, HEAD_WIDTH).astype(jnp.float32)).astype(jnp.bfloat16)
        out_list.append(jnp.sum(blocks.astype(jnp.float32), axis=0))
        value_list.append(lax.dot_general(tokens, value_gradient, (((0,), (0,)), ((), ())), preferred_element_type=jnp.float32))
        input_list.append(result)
        incoming = result
    grad_input = jnp.stack(input_list[::-1])
    grad_value = jnp.stack(value_list[::-1])
    grad_out = jnp.stack(out_list[::-1])
    return grad_input, grad_value, grad_out
```

```python
import functools

import jax
import jax.numpy as jnp
from jax import lax
from jax.experimental import pallas as pl
from jax.experimental.pallas import tpu as pltpu
from jax.sharding import PartitionSpec as P

MESH = pl.DeviceIdType.MESH
F32 = jnp.float32
BF16 = jnp.bfloat16


def masked_probs(logits, doc_ids):
    seq_len = logits.shape[-1]
    places = jnp.arange(seq_len)
    allowed = (places[None, :, None] >= places[None, None, :]) & (
        doc_ids[:, :, None] == doc_ids[:, None, :]
    )
    kept = jnp.where(allowed, logits, -jnp.inf)
    row_top = jnp.max(kept, axis=-1, keepdims=True)
    expo = jnp.where(allowed, jnp.exp(kept - row_top), jnp.zeros_like(logits))
    return (expo / jnp.sum(expo, axis=-1, keepdims=True)).astype(BF16)


def chain_kernel(
    n_z,
    chunk_count,
    heads_ref,
    probs_ref,
    cross_ref,
    spread_ref,
    cot_ref,
    grad_ref,
    above_ref,
    middle_ref,
    backs_ref,
    line,
    below,
    other,
    delta_low,
    delta_mid,
    line_send,
    line_recv,
    pair_send,
    pair_recv,
    wave_send,
    wave_recv,
    out_send,
    out_recv,
    cot_sem,
):
    section = lax.axis_index("section")
    z, side = section // 2, section % 2
    rows, width = heads_ref.shape
    head = width // 2
    chunk = spread_ref.shape[2]
    half = chunk * chunk_count
    lower = {"section": lax.rem(z + n_z - 1, n_z) * 2 + side}
    upper = {"section": lax.rem(z + 1, n_z) * 2 + side}
    partner = {"section": z * 2 + 1 - side}

    barrier = pltpu.get_barrier_semaphore()
    for device in (lower, upper, partner):
        pl.semaphore_signal(barrier, inc=1, device_id=device, device_id_type=MESH)
    pl.semaphore_wait(barrier, 3)

    def cot_copy(k):
        columns = pl.ds(pl.multiple_of(side * half + k * chunk, 128), chunk)
        return pltpu.make_async_copy(cot_ref.at[:, columns], above_ref.at[k], cot_sem.at[k])

    @pl.when(z == n_z - 1)
    def _():
        for k in range(chunk_count):
            cot_copy(k).start()

    def line_copy(slot):
        return pltpu.make_async_remote_copy(
            src_ref=line.at[slot],
            dst_ref=line.at[slot],
            send_sem=line_send.at[slot],
            recv_sem=line_recv.at[slot],
            device_id=lower,
            device_id_type=MESH,
        )

    def wave_copy(k):
        return pltpu.make_async_remote_copy(
            src_ref=below.at[k],
            dst_ref=above_ref.at[k],
            send_sem=wave_send.at[k],
            recv_sem=wave_recv.at[k],
            device_id=lower,
            device_id_type=MESH,
        )

    def out_copy(k):
        columns = pl.ds(pl.multiple_of(side * half + k * chunk, 128), chunk)
        return pltpu.make_async_remote_copy(
            src_ref=other.at[k],
            dst_ref=grad_ref.at[:, columns],
            send_sem=out_send.at[k],
            recv_sem=out_recv.at[k],
            device_id=partner,
            device_id_type=MESH,
        )

    def take(i, total):
        slot = n_z - 1 - i
        line_copy(slot).wait_recv()

        @pl.when(z > 0)
        def _():
            line_copy(slot).start()

        return total + jnp.dot(line[slot], cross_ref[slot], preferred_element_type=F32)

    total = lax.fori_loop(0, n_z - 1 - z, take, heads_ref[...])
    back_top = jnp.dot(
        probs_ref[1], total[:, head:].astype(BF16), preferred_element_type=F32
    ).astype(BF16)
    low = total[:, :head] + jnp.dot(
        back_top, cross_ref[z, head:, :head], preferred_element_type=F32
    )
    back_low = jnp.dot(probs_ref[0], low.astype(BF16), preferred_element_type=F32).astype(BF16)
    line[z, :, :head] = back_low
    line[z, :, head:] = back_top

    @pl.when(z > 0)
    def _():
        line_copy(z).start()

    own_rows = pl.ds(pl.multiple_of(side * rows, rows), rows)
    backs_ref[own_rows, :head] = back_low
    backs_ref[own_rows, head:] = back_top
    swap = pltpu.make_async_remote_copy(
        src_ref=backs_ref.at[own_rows],
        dst_ref=backs_ref.at[own_rows],
        send_sem=pair_send,
        recv_sem=pair_recv,
        device_id=partner,
        device_id_type=MESH,
    )
    swap.start()
    swap.wait_send()
    other_rows = pl.ds(pl.multiple_of((1 - side) * rows, rows), rows)
    pltpu.make_async_remote_copy(
        src_ref=backs_ref.at[own_rows],
        dst_ref=backs_ref.at[other_rows],
        send_sem=pair_send,
        recv_sem=pair_recv,
        device_id=partner,
        device_id_type=MESH,
    ).wait_recv()

    for k in range(chunk_count):
        delta_low[k] = jnp.dot(backs_ref[...], spread_ref[k], preferred_element_type=F32)
        delta_mid[k] = jnp.dot(
            backs_ref[:, head:], spread_ref[k, head:, :], preferred_element_type=F32
        )

    for k in range(chunk_count):

        @pl.when(z == n_z - 1)
        def _():
            cot_copy(k).wait()

        @pl.when(z < n_z - 1)
        def _():
            wave_copy(k).wait_recv()

        above = above_ref[k].astype(F32)
        low = (above + delta_low[k]).astype(BF16)
        middle = (above + delta_mid[k]).astype(BF16)
        below[k] = low

        @pl.when(z > 0)
        def _():
            wave_copy(k).start()

        middle_ref[k] = middle
        columns = pl.ds(pl.multiple_of(side * half + k * chunk, 128), chunk)
        grad_ref[:, columns] = jnp.where(side == 1, middle, low)
        other[k] = jnp.where(side == 1, low, middle)
        out_copy(k).start()

    for k in range(chunk_count):
        out_copy(k).wait_send()
        columns = pl.ds(pl.multiple_of((1 - side) * half + k * chunk, 128), chunk)
        pltpu.make_async_remote_copy(
            src_ref=other.at[k],
            dst_ref=grad_ref.at[:, columns],
            send_sem=out_send.at[k],
            recv_sem=out_recv.at[k],
            device_id=partner,
            device_id_type=MESH,
        ).wait_recv()

    @pl.when(z > 0)
    def _():
        for k in range(chunk_count):
            wave_copy(k).wait_send()

        def drain(i, carry):
            line_copy(n_z - 1 - i).wait_send()
            return carry

        lax.fori_loop(0, n_z - z, drain, 0)


def scatter_kernel(n_dp, out_ref, value_ref, sum_out_ref, sum_value_ref, got_out, got_value, out_send, out_recv, value_send, value_recv):
    section = lax.axis_index("section")
    me = lax.axis_index("dp")
    z, side = section // 2, section % 2
    rows = sum_out_ref.shape[0]
    half_dp = n_dp // 2
    source = me // half_dp

    barrier = pltpu.get_barrier_semaphore()
    for other in (0, 1):
        for step in range(n_dp):
            if other or step:
                pl.semaphore_signal(
                    barrier,
                    inc=1,
                    device_id={"section": z * 2 + (side + other) % 2, "dp": lax.rem(me + step, n_dp)},
                    device_id_type=MESH,
                )
    pl.semaphore_wait(barrier, 2 * n_dp - 1)

    def value_copy(step, to):
        return pltpu.make_async_remote_copy(
            src_ref=value_ref.at[pl.ds(pl.multiple_of(to * rows, 16), rows)],
            dst_ref=got_value.at[step],
            send_sem=value_send.at[step],
            recv_sem=value_recv.at[step],
            device_id={"section": section, "dp": to},
            device_id_type=MESH,
        )

    def out_copy(layer, i):
        return pltpu.make_async_remote_copy(
            src_ref=out_ref.at[layer, pl.ds(i * rows, rows)],
            dst_ref=got_out.at[me],
            send_sem=out_send.at[layer, i],
            recv_sem=out_recv.at[me],
            device_id={"section": z * 2 + layer, "dp": side * half_dp + i},
            device_id_type=MESH,
        )

    def self_copy(i):
        return pltpu.make_async_copy(out_ref.at[side, pl.ds(i * rows, rows)], got_out.at[me], out_recv.at[me])

    for layer in (0, 1):
        for i in range(half_dp):
            own = (layer == side) & (side * half_dp + i == me)

            @pl.when(jnp.logical_not(own))
            def _():
                out_copy(layer, i).start()

            @pl.when(own)
            def _():
                self_copy(i).start()

    for step in range(1, n_dp):
        value_copy(step, lax.rem(me + step, n_dp)).start()

    total = value_ref[pl.ds(pl.multiple_of(me * rows, 16), rows)].astype(F32)
    for step in range(1, n_dp):
        value_copy(step, lax.rem(me + step, n_dp)).wait_recv()
        total = total + got_value[step].astype(F32)
    sum_value_ref[...] = total

    for peer in range(n_dp):
        own = (source == side) & (peer == me)

        @pl.when(jnp.logical_not(own))
        def _():
            pltpu.make_async_remote_copy(
                src_ref=out_ref.at[0, pl.ds(0, rows)],
                dst_ref=got_out.at[peer],
                send_sem=out_send.at[0, 0],
                recv_sem=out_recv.at[peer],
                device_id={"section": z * 2 + source, "dp": peer},
                device_id_type=MESH,
            ).wait_recv()

        @pl.when(own)
        def _():
            self_copy(0).wait()

    total = got_out[0].astype(F32)
    for peer in range(1, n_dp):
        total = total + got_out[peer].astype(F32)
    sum_out_ref[...] = total

    for step in range(1, n_dp):
        value_copy(step, lax.rem(me + step, n_dp)).wait_send()
    for layer in (0, 1):
        for i in range(half_dp):
            own = (layer == side) & (side * half_dp + i == me)

            @pl.when(jnp.logical_not(own))
            def _():
                out_copy(layer, i).wait_send()


def shards(acts, scores, segments, cotangent, w_value, w_out):
    n_section = lax.axis_size("section")
    n_dp = lax.axis_size("dp")
    n_z = n_section // 2
    section = lax.axis_index("section")
    side = section % 2
    tokens = acts[0]
    row_count, feat_width = tokens.shape
    micro_count, seq_len = segments.shape
    shard_rows, head = w_value.shape[1:]
    half = feat_width // 2
    chunk = 256 if half % 256 == 0 else 128
    chunk_count = half // chunk

    def swapped(array):
        return lax.ppermute(array, "section", [(i, i ^ 1) for i in range(n_section)])

    def ordered(mine, others, axis):
        return jnp.where(
            side == 0,
            jnp.concatenate([mine, others], axis),
            jnp.concatenate([others, mine], axis),
        )

    value_full = lax.all_gather(w_value[0], "dp", axis=0, tiled=True)
    out_full = lax.all_gather(w_out[0], "dp", axis=0, tiled=True)
    value_layers = lax.all_gather(w_value[0], "section", axis=0)
    cross = lax.psum(
        jnp.einsum("tdk,dj->tkj", value_layers, w_out[0], preferred_element_type=F32).astype(BF16),
        "dp",
    ).reshape(n_z, 2 * head, head)
    cross = ordered(cross, swapped(cross), 2)

    probs = masked_probs(scores[0], segments)
    probs_turned = jnp.swapaxes(probs, 1, 2)
    projected = jnp.dot(tokens, value_full, preferred_element_type=F32).astype(BF16)
    mixed = jnp.einsum(
        "xzj,xjs->xzs",
        probs,
        projected.reshape(micro_count, seq_len, head),
        preferred_element_type=F32,
    ).astype(BF16).reshape(row_count, head)
    heads = jnp.dot(cotangent, out_full, preferred_element_type=F32).reshape(micro_count, seq_len, head)

    def picked(array, index):
        return lax.dynamic_index_in_dim(array, index, 0, keepdims=False)

    heads = ordered(picked(heads, side), swapped(picked(heads, 1 - side)), 1)
    turned = ordered(picked(probs_turned, side)[None], swapped(picked(probs_turned, 1 - side))[None], 0)
    halves = value_full.reshape(2, half, head)
    spread = ordered(picked(halves, side), swapped(picked(halves, 1 - side)), 1)
    spread = jnp.swapaxes(spread.reshape(chunk_count, chunk, 2 * head), 1, 2)
    mixed_pair = ordered(mixed[None], swapped(mixed)[None], 0)

    vmem = pl.BlockSpec(memory_space=pltpu.VMEM)
    grad_input, above, middle, backs = pl.pallas_call(
        functools.partial(chain_kernel, n_z, chunk_count),
        out_shape=(
            jax.ShapeDtypeStruct((row_count, feat_width), BF16),
            jax.ShapeDtypeStruct((chunk_count, row_count, chunk), BF16),
            jax.ShapeDtypeStruct((chunk_count, row_count, chunk), BF16),
            jax.ShapeDtypeStruct((row_count, 2 * head), BF16),
        ),
        in_specs=[vmem] * 4 + [pl.BlockSpec(memory_space=pl.ANY)],
        out_specs=(vmem,) * 4,
        scratch_shapes=[
            pltpu.VMEM((n_z, seq_len, 2 * head), BF16),
            pltpu.VMEM((chunk_count, row_count, chunk), BF16),
            pltpu.VMEM((chunk_count, row_count, chunk), BF16),
            pltpu.VMEM((chunk_count, row_count, chunk), F32),
            pltpu.VMEM((chunk_count, row_count, chunk), F32),
            pltpu.SemaphoreType.DMA((n_z,)),
            pltpu.SemaphoreType.DMA((n_z,)),
            pltpu.SemaphoreType.DMA,
            pltpu.SemaphoreType.DMA,
            pltpu.SemaphoreType.DMA((chunk_count,)),
            pltpu.SemaphoreType.DMA((chunk_count,)),
            pltpu.SemaphoreType.DMA((chunk_count,)),
            pltpu.SemaphoreType.DMA((chunk_count,)),
            pltpu.SemaphoreType.DMA((chunk_count,)),
        ],
        compiler_params=pltpu.CompilerParams(
            collective_id=0, has_side_effects=True, vmem_limit_bytes=48 << 20
        ),
        name="chain",
    )(heads, turned, cross, spread, cotangent)

    out_parts = jnp.stack(
        [
            jnp.einsum("ctd,th->cdh", middle, mixed_pair[0], preferred_element_type=F32),
            jnp.einsum("ctd,th->cdh", above, mixed_pair[1], preferred_element_type=F32),
        ]
    ).astype(BF16).reshape(2, half, head)
    own_back = picked(jnp.stack([backs[:, :head], backs[:, head:]]), side)
    value_parts = lax.dot_general(
        tokens, own_back, (((0,), (0,)), ((), ())), preferred_element_type=F32
    ).astype(BF16)

    grad_out, grad_value = pl.pallas_call(
        functools.partial(scatter_kernel, n_dp),
        out_shape=(jax.ShapeDtypeStruct((shard_rows, head), F32),) * 2,
        in_specs=[vmem] * 2,
        out_specs=(vmem,) * 2,
        scratch_shapes=[
            pltpu.VMEM((n_dp, shard_rows, head), BF16),
            pltpu.VMEM((n_dp, shard_rows, head), BF16),
            pltpu.SemaphoreType.DMA((2, n_dp // 2)),
            pltpu.SemaphoreType.DMA((n_dp,)),
            pltpu.SemaphoreType.DMA((n_dp,)),
            pltpu.SemaphoreType.DMA((n_dp,)),
        ],
        compiler_params=pltpu.CompilerParams(
            collective_id=1, has_side_effects=True, vmem_limit_bytes=48 << 20
        ),
        name="scatter",
    )(out_parts, value_parts)
    return (grad_input[None], grad_value[None], grad_out[None])


def solution(mesh):
    placed = (
        P("section", "dp", None),
        P("section", "dp", None, None),
        P("dp", None),
        P("dp", None),
        P("section", "dp", None),
        P("section", "dp", None),
    )
    return jax.shard_map(
        shards,
        mesh=mesh,
        in_specs=placed,
        out_specs=(P("section", "dp", None), P("section", "dp", None), P("section", "dp", None)),
        check_vma=False,
    )
```

```python
import functools

import jax
import jax.numpy as jnp
from jax import lax
from jax.experimental import pallas as pl
from jax.experimental.pallas import tpu as pltpu
from jax.sharding import PartitionSpec as P

MESH = pl.DeviceIdType.MESH
F32 = jnp.float32
BF16 = jnp.bfloat16


def masked_probs(logits, doc_ids):
    seq_len = logits.shape[-1]
    places = jnp.arange(seq_len)
    allowed = (places[None, :, None] >= places[None, None, :]) & (
        doc_ids[:, :, None] == doc_ids[:, None, :]
    )
    kept = jnp.where(allowed, logits, -jnp.inf)
    row_top = jnp.max(kept, axis=-1, keepdims=True)
    expo = jnp.where(allowed, jnp.exp(kept - row_top), jnp.zeros_like(logits))
    return (expo / jnp.sum(expo, axis=-1, keepdims=True)).astype(BF16)


def dot(a, b):
    return jnp.dot(a, b, preferred_element_type=F32)


def dot_rows(a, b):
    return lax.dot_general(a, b, (((0,), (0,)), ((), ())), preferred_element_type=F32)


def dot_lanes(a, b):
    return lax.dot_general(a, b, (((1,), (1,)), ((), ())), preferred_element_type=F32)


def kernel(
    n_z,
    n_dp,
    chunk,
    acts_ref,
    cot_ref,
    turned_ref,
    value_ref,
    outw_ref,
    grad_ref,
    sum_value_ref,
    sum_out_ref,
    out_full,
    pair_rows,
    rest_rows,
    pair_out,
    layer_rows,
    part,
    parts_in,
    cross,
    heads,
    head_away,
    turned,
    line,
    backs,
    mixed,
    delta_low,
    delta_mid,
    above,
    below,
    middle,
    other,
    out_parts,
    value_parts,
    out_in,
    value_in,
    pair_out_s,
    pair_out_r,
    turned_s,
    turned_r,
    head_s,
    head_r,
    mixed_s,
    mixed_r,
    backs_s,
    backs_r,
    layer_s,
    layer_r,
    outw_s,
    outw_r,
    value_s,
    value_r,
    near_s,
    near_r,
    part_s,
    part_r,
    cross_s,
    cross_r,
    line_s,
    line_r,
    wave_s,
    wave_r,
    grad_s,
    grad_r,
    vsum_s,
    vsum_r,
    osum_s,
    osum_r,
):
    section = lax.axis_index("section")
    me = lax.axis_index("dp")
    z, side = section // 2, section % 2
    away = 1 - side
    half_dp = n_dp // 2
    my_half, my_place = me // half_dp, me % half_dp
    rows, head = value_ref.shape
    half = rows * half_dp
    chunk_count = half // chunk
    seq = heads.shape[0]
    lower = {"section": lax.rem(z + n_z - 1, n_z) * 2 + side}
    upper = {"section": lax.rem(z + 1, n_z) * 2 + side}
    partner = {"section": z * 2 + away}
    own_lanes = pl.ds(pl.multiple_of(side * head, head), head)
    away_lanes = pl.ds(pl.multiple_of(away * head, head), head)
    own_seq = pl.ds(pl.multiple_of(side * seq, seq), seq)
    away_seq = pl.ds(pl.multiple_of(away * seq, seq), seq)

    def peer(step):
        return lax.rem(me + step, n_dp)

    def shard(place):
        return pl.ds(pl.multiple_of(place * rows, 16), rows)

    def remote(src, dst, send, recv, device):
        return pltpu.make_async_remote_copy(
            src_ref=src, dst_ref=dst, send_sem=send, recv_sem=recv, device_id=device, device_id_type=MESH
        )

    barrier = pltpu.get_barrier_semaphore()
    for device in (lower, upper):
        pl.semaphore_signal(barrier, inc=1, device_id=device, device_id_type=MESH)

    def greet(step, carry):
        for target in (0, 1):
            @pl.when((target != side) | (step > 0))
            def _():
                pl.semaphore_signal(
                    barrier, inc=1, device_id={"section": z * 2 + target, "dp": peer(step)}, device_id_type=MESH
                )
        return carry

    lax.fori_loop(0, n_dp, greet, 0)
    pl.semaphore_wait(barrier, 2 * n_dp + 1)

    pair_copy = remote(outw_ref, pair_out.at[:, own_lanes], pair_out_s, pair_out_r, partner)
    pair_copy.start()

    def layer_copy(slot, src):
        return remote(src, layer_rows.at[slot], layer_s.at[slot], layer_r.at[slot], lower)

    @pl.when(z > 0)
    def _():
        layer_copy(z, value_ref).start()

    def outw_copy(step):
        return remote(outw_ref, out_full.at[shard(me)], outw_s.at[step], outw_r.at[step], {"dp": peer(step)})

    def value_copy(step, inside):
        dst = pair_rows.at[shard(my_place), own_lanes] if inside else rest_rows.at[shard(my_place)]
        return remote(value_ref, dst, value_s.at[step], value_r.at[step], {"dp": peer(step)})

    def near_copy(step):
        return remote(
            value_ref,
            pair_rows.at[shard(my_place), own_lanes],
            near_s.at[step],
            near_r.at[my_place],
            {"section": z * 2 + away, "dp": peer(step)},
        )

    def each_step(first, do):
        def body(step, carry):
            do(step)
            return carry

        lax.fori_loop(first, n_dp, body, 0)

    def start_value(step):
        @pl.when(my_half == side)
        def _():
            value_copy(step, True).start()

        @pl.when(my_half != side)
        def _():
            value_copy(step, False).start()

    each_step(1, lambda step: outw_copy(step).start())
    turned_copy = remote(turned_ref.at[away], turned.at[side], turned_s, turned_r, partner)
    turned_copy.start()
    each_step(1, start_value)

    @pl.when(my_half == away)
    def _():
        each_step(0, lambda step: near_copy(step).start())

    turned[side] = turned_ref[side]
    out_full[shard(me)] = outw_ref[...]
    pair_out[:, own_lanes] = outw_ref[...]
    layer_rows[z] = value_ref[...]

    @pl.when(my_half == side)
    def _():
        pair_rows[shard(my_place), own_lanes] = value_ref[...]

    @pl.when(my_half != side)
    def _():
        rest_rows[shard(my_place)] = value_ref[...]

    remote(outw_ref, pair_out.at[:, away_lanes], pair_out_s, pair_out_r, partner).wait_recv()

    def part_copy(slot):
        return remote(part.at[slot], parts_in.at[me], part_s.at[slot], part_r.at[me], {"dp": slot})

    def cross_copy(step, target):
        block = cross.at[me, own_lanes]
        return remote(
            block,
            block,
            cross_s.at[target * n_dp + step],
            cross_r.at[2 * me + side],
            {"section": z * 2 + target, "dp": peer(step)},
        )

    def each_cross(do):
        for target in (0, 1):
            def at(step, target=target):
                @pl.when((target != side) | (step > 0))
                def _():
                    do(cross_copy(step, target))

            each_step(0, at)

    def sum_parts():
        def add(step, total):
            source = peer(step)
            remote(part.at[0], parts_in.at[source], part_s.at[0], part_r.at[source], {"dp": source}).wait_recv()
            return total + parts_in[source].astype(F32)

        total = lax.fori_loop(1, n_dp, add, part[me].astype(F32))
        cross[me, own_lanes] = total.astype(BF16)
        each_cross(lambda copy: copy.start())

    def cross_part(slot, carry):
        @pl.when(slot > z)
        def _():
            layer_copy(slot, layer_rows.at[slot]).wait_recv()

            @pl.when(z > 0)
            def _():
                layer_copy(slot, layer_rows.at[slot]).start()

        part[slot] = dot_rows(layer_rows[slot], pair_out[...]).astype(BF16)

        @pl.when(me != slot)
        def _():
            part_copy(slot).start()

        @pl.when((slot > z) & (me == slot - 1))
        def _():
            sum_parts()

        return carry

    lax.fori_loop(z, n_z, cross_part, 0)

    @pl.when(me == n_z - 1)
    def _():
        sum_parts()

    def outw_wait(step):
        source = lax.rem(me + n_dp - step, n_dp)
        remote(outw_ref, out_full.at[shard(source)], outw_s.at[step], outw_r.at[step], {"dp": source}).wait_recv()

    each_step(1, outw_wait)
    own_heads = dot(cot_ref[...], out_full[...])
    backs_f32 = jnp.where(side == 0, own_heads[:seq], own_heads[seq:])
    heads[:, own_lanes] = backs_f32
    head_away[...] = jnp.where(side == 0, own_heads[seq:], own_heads[:seq])
    head_copy = remote(head_away, heads.at[:, own_lanes], head_s, head_r, partner)
    head_copy.start()
    remote(head_away, heads.at[:, away_lanes], head_s, head_r, partner).wait_recv()
    remote(turned_ref.at[side], turned.at[away], turned_s, turned_r, partner).wait_recv()

    def line_copy(slot):
        return remote(line.at[slot], line.at[slot], line_s.at[slot], line_r.at[slot], lower)

    def cross_wait(slot):
        for target in (0, 1):
            @pl.when((target != side) | (me != slot))
            def _():
                block = cross.at[slot, pl.ds(target * head, head)]
                remote(block, block, cross_s.at[0], cross_r.at[2 * slot + target], partner).wait_recv()

    def take(i, total):
        slot = n_z - 1 - i
        line_copy(slot).wait_recv()

        @pl.when(z > 0)
        def _():
            line_copy(slot).start()

        cross_wait(slot)
        return total + dot(line[slot], cross[slot])

    total = lax.fori_loop(0, n_z - 1 - z, take, heads[...])
    back_top = dot(turned[1, :, :seq], total[:, head:].astype(BF16)).astype(BF16)
    cross_wait(z)
    low_head = total[:, :head] + dot(back_top, cross[z, head:, :head])
    back_low = dot(turned[0, :, :seq], low_head.astype(BF16)).astype(BF16)
    line[z, :, :head] = back_low
    line[z, :, head:] = back_top

    @pl.when(z > 0)
    def _():
        line_copy(z).start()

    backs[own_seq, :head] = back_low
    backs[own_seq, head:] = back_top
    backs_copy = remote(line.at[z], backs.at[own_seq], backs_s, backs_r, partner)
    backs_copy.start()
    remote(line.at[z], backs.at[away_seq], backs_s, backs_r, partner).wait_recv()

    def value_wait(step):
        source = lax.rem(me + n_dp - step, n_dp)
        place = shard(lax.rem(source, half_dp))

        @pl.when(source // half_dp == side)
        def _():
            dst = pair_rows.at[place, own_lanes]
            remote(value_ref, dst, value_s.at[step], value_r.at[step], {"dp": source}).wait_recv()

        @pl.when(source // half_dp != side)
        def _():
            dst = rest_rows.at[place]
            remote(value_ref, dst, value_s.at[step], value_r.at[step], {"dp": source}).wait_recv()

    each_step(1, value_wait)
    for place in range(half_dp):
        dst = pair_rows.at[pl.ds(place * rows, rows), away_lanes]
        remote(value_ref, dst, near_s.at[0], near_r.at[place], partner).wait_recv()

    for k in range(chunk_count):
        weights = pair_rows[pl.ds(k * chunk, chunk), :]
        delta_low[k] = dot_lanes(backs[...], weights)
        delta_mid[k] = dot_lanes(backs[:, head:], weights[:, head:])

    def half_lanes(which):
        return pl.ds(pl.multiple_of(which * half, 128), half)

    projected = (
        dot(acts_ref[:, half_lanes(side)], pair_rows[:, own_lanes]) + dot(acts_ref[:, half_lanes(away)], rest_rows[...])
    ).astype(BF16)
    mixed[side, :seq] = dot_rows(turned_ref[0, :, :seq], projected[:seq]).astype(BF16)
    mixed[side, seq:] = dot_rows(turned_ref[1, :, :seq], projected[seq:]).astype(BF16)
    mixed_copy = remote(mixed.at[side], mixed.at[side], mixed_s, mixed_r, partner)
    mixed_copy.start()

    def vsum_copy(step):
        return remote(
            value_parts.at[shard(peer(step))], value_in.at[step], vsum_s.at[step], vsum_r.at[step], {"dp": peer(step)}
        )

    def value_gradient():
        own_back = backs[:, own_lanes]

        def piece(k, carry):
            start = pl.multiple_of(k * chunk, 128)
            value_parts[pl.ds(start, chunk)] = dot_rows(acts_ref[:, pl.ds(start, chunk)], own_back).astype(BF16)
            return carry

        lax.fori_loop(0, 2 * chunk_count, piece, 0)
        each_step(1, lambda step: vsum_copy(step).start())

    @pl.when(z < n_z - 1)
    def _():
        value_gradient()

    remote(mixed.at[side], mixed.at[away], mixed_s, mixed_r, partner).wait_recv()

    def wave_copy(k):
        return remote(below.at[k], above.at[k], wave_s.at[k], wave_r.at[k], lower)

    def columns(which, k):
        return pl.ds(pl.multiple_of(which * half + k * chunk, 128), chunk)

    def grad_copy(k):
        return remote(other.at[k], grad_ref.at[:, columns(side, k)], grad_s.at[k], grad_r.at[k], partner)

    def osum_copy(layer, i):
        return remote(
            out_parts.at[layer, pl.ds(i * rows, rows)],
            out_in.at[me],
            osum_s.at[layer * half_dp + i],
            osum_r.at[me],
            {"section": z * 2 + layer, "dp": side * half_dp + i},
        )

    def is_own(layer, i):
        return (layer == side) & (side * half_dp + i == me)

    def osum_start(layer, i):
        @pl.when(jnp.logical_not(is_own(layer, i)))
        def _():
            osum_copy(layer, i).start()

        @pl.when(is_own(layer, i))
        def _():
            out_in[me] = out_parts[layer, pl.ds(i * rows, rows)]

    sent = 0
    for k in range(chunk_count):
        @pl.when(z == n_z - 1)
        def _():
            above[k] = cot_ref[:, columns(side, k)]

        @pl.when(z < n_z - 1)
        def _():
            wave_copy(k).wait_recv()

        taken = above[k]
        low = (taken.astype(F32) + delta_low[k]).astype(BF16)
        below[k] = low

        @pl.when(z > 0)
        def _():
            wave_copy(k).start()

        mid = (taken.astype(F32) + delta_mid[k]).astype(BF16)
        grad_ref[:, columns(side, k)] = jnp.where(side == 1, mid, low)
        other[k] = jnp.where(side == 1, low, mid)
        grad_copy(k).start()
        out_parts[0, pl.ds(k * chunk, chunk)] = dot_rows(mid, mixed[0]).astype(BF16)
        out_parts[1, pl.ds(k * chunk, chunk)] = dot_rows(taken, mixed[1]).astype(BF16)
        while (sent + 1) * rows <= (k + 1) * chunk:
            for layer in (0, 1):
                osum_start(layer, sent)
            sent += 1

    @pl.when(z == n_z - 1)
    def _():
        value_gradient()

    total = value_parts[shard(me)].astype(F32)
    for step in range(1, n_dp):
        remote(
            value_parts.at[pl.ds(0, rows)], value_in.at[step], vsum_s.at[step], vsum_r.at[step], {"dp": peer(step)}
        ).wait_recv()
        total = total + value_in[step].astype(F32)
    sum_value_ref[...] = total

    source_line = z * 2 + my_half
    total = jnp.zeros((rows, head), F32)
    for source in range(n_dp):
        @pl.when((my_half != side) | (source != me))
        def _():
            remote(
                out_parts.at[0, pl.ds(0, rows)],
                out_in.at[source],
                osum_s.at[0],
                osum_r.at[source],
                {"section": source_line, "dp": source},
            ).wait_recv()

        total = total + out_in[source].astype(F32)
    sum_out_ref[...] = total

    for k in range(chunk_count):
        grad_copy(k).wait_send()
        remote(other.at[k], grad_ref.at[:, columns(away, k)], grad_s.at[k], grad_r.at[k], partner).wait_recv()

    pair_copy.wait_send()
    turned_copy.wait_send()
    head_copy.wait_send()
    backs_copy.wait_send()
    mixed_copy.wait_send()
    each_step(1, lambda step: outw_copy(step).wait_send())
    each_step(1, lambda step: vsum_copy(step).wait_send())

    def value_sent(step):
        @pl.when(my_half == side)
        def _():
            value_copy(step, True).wait_send()

        @pl.when(my_half != side)
        def _():
            value_copy(step, False).wait_send()

    each_step(1, value_sent)

    @pl.when(my_half == away)
    def _():
        each_step(0, lambda step: near_copy(step).wait_send())

    def part_sent(slot, carry):
        @pl.when(me != slot)
        def _():
            part_copy(slot).wait_send()

        return carry

    lax.fori_loop(z, n_z, part_sent, 0)

    @pl.when((me >= z) & (me < n_z))
    def _():
        each_cross(lambda copy: copy.wait_send())

    for layer in (0, 1):
        for i in range(half_dp):
            @pl.when(jnp.logical_not(is_own(layer, i)))
            def _():
                osum_copy(layer, i).wait_send()

    @pl.when(z > 0)
    def _():
        layer_copy(z, value_ref).wait_send()

        def layer_sent(slot, carry):
            layer_copy(slot, layer_rows.at[slot]).wait_send()
            return carry

        lax.fori_loop(z + 1, n_z, layer_sent, 0)

        def line_sent(slot, carry):
            line_copy(slot).wait_send()
            return carry

        lax.fori_loop(z, n_z, line_sent, 0)
        for k in range(chunk_count):
            wave_copy(k).wait_send()


def shards(acts, scores, segments, cotangent, w_value, w_out):
    n_dp = lax.axis_size("dp")
    n_z = lax.axis_size("section") // 2
    tokens = acts[0]
    row_count, feat_width = tokens.shape
    seq_len = segments.shape[1]
    shard_rows, head = w_value.shape[1:]
    half = feat_width // 2
    chunk = 256 if half % 256 == 0 else 128
    chunks = half // chunk

    probs = masked_probs(scores[0], segments)
    turned = jnp.pad(jnp.swapaxes(probs, 1, 2), ((0, 0), (0, 0), (0, 128 - seq_len)))

    vmem = pl.BlockSpec(memory_space=pltpu.VMEM)
    dma = pltpu.SemaphoreType.DMA
    one, per_z, per_dp, per_chunk = dma, dma((n_z,)), dma((n_dp,)), dma((chunks,))
    grad_input, grad_value, grad_out = pl.pallas_call(
        functools.partial(kernel, n_z, n_dp, chunk),
        out_shape=(
            jax.ShapeDtypeStruct((row_count, feat_width), BF16),
            jax.ShapeDtypeStruct((shard_rows, head), F32),
            jax.ShapeDtypeStruct((shard_rows, head), F32),
        ),
        in_specs=[vmem] * 5,
        out_specs=(vmem,) * 3,
        scratch_shapes=[
            pltpu.VMEM((feat_width, head), BF16),
            pltpu.VMEM((half, 2 * head), BF16),
            pltpu.VMEM((half, head), BF16),
            pltpu.VMEM((shard_rows, 2 * head), BF16),
            pltpu.VMEM((n_z, shard_rows, head), BF16),
            pltpu.VMEM((n_z, head, 2 * head), BF16),
            pltpu.VMEM((n_dp, head, 2 * head), BF16),
            pltpu.VMEM((n_z, 2 * head, 2 * head), BF16),
            pltpu.VMEM((seq_len, 2 * head), F32),
            pltpu.VMEM((seq_len, head), F32),
            pltpu.VMEM((2, seq_len, 128), BF16),
            pltpu.VMEM((n_z, seq_len, 2 * head), BF16),
            pltpu.VMEM((row_count, 2 * head), BF16),
            pltpu.VMEM((2, row_count, head), BF16),
            pltpu.VMEM((chunks, row_count, chunk), F32),
            pltpu.VMEM((chunks, row_count, chunk), F32),
            pltpu.VMEM((chunks, row_count, chunk), BF16),
            pltpu.VMEM((chunks, row_count, chunk), BF16),
            pltpu.VMEM((8, 128), BF16),
            pltpu.VMEM((chunks, row_count, chunk), BF16),
            pltpu.VMEM((2, half, head), BF16),
            pltpu.VMEM((feat_width, head), BF16),
            pltpu.VMEM((n_dp, shard_rows, head), BF16),
            pltpu.VMEM((n_dp, shard_rows, head), BF16),
            *([one] * 10),
            per_z,
            per_z,
            per_dp,
            per_dp,
            per_dp,
            per_dp,
            per_dp,
            dma((n_dp // 2,)),
            per_z,
            per_dp,
            dma((2 * n_dp,)),
            dma((2 * n_z,)),
            per_z,
            per_z,
            per_chunk,
            per_chunk,
            per_chunk,
            per_chunk,
            per_dp,
            per_dp,
            per_dp,
            per_dp,
        ],
        compiler_params=pltpu.CompilerParams(
            collective_id=0, has_side_effects=True, vmem_limit_bytes=52 << 20
        ),
        name="backward",
    )(tokens, cotangent, turned, w_value[0], w_out[0])
    return (grad_input[None], grad_value[None], grad_out[None])


def solution(mesh):
    placed = (
        P("section", "dp", None),
        P("section", "dp", None, None),
        P("dp", None),
        P("dp", None),
        P("section", "dp", None),
        P("section", "dp", None),
    )
    return jax.shard_map(
        shards,
        mesh=mesh,
        in_specs=placed,
        out_specs=(P("section", "dp", None), P("section", "dp", None), P("section", "dp", None)),
        check_vma=False,
    )
```

```python
import functools

import jax
import jax.numpy as jnp
from jax import lax
from jax.experimental import pallas as pl
from jax.experimental.pallas import tpu as pltpu
from jax.sharding import PartitionSpec as P

MESH = pl.DeviceIdType.MESH
F32 = jnp.float32
BF16 = jnp.bfloat16


def masked_probs(logits, doc_ids):
    seq_len = logits.shape[-1]
    places = jnp.arange(seq_len)
    allowed = (places[None, :, None] >= places[None, None, :]) & (
        doc_ids[:, :, None] == doc_ids[:, None, :]
    )
    kept = jnp.where(allowed, logits, -jnp.inf)
    row_top = jnp.max(kept, axis=-1, keepdims=True)
    expo = jnp.where(allowed, jnp.exp(kept - row_top), jnp.zeros_like(logits))
    return (expo / jnp.sum(expo, axis=-1, keepdims=True)).astype(BF16)


def dot(a, b):
    return jnp.dot(a, b, preferred_element_type=F32)


def dot_rows(a, b):
    return lax.dot_general(a, b, (((0,), (0,)), ((), ())), preferred_element_type=F32)


def dot_lanes(a, b):
    return lax.dot_general(a, b, (((1,), (1,)), ((), ())), preferred_element_type=F32)


def kernel(
    n_z,
    n_dp,
    chunk,
    acts_ref,
    cot_ref,
    turned_ref,
    value_ref,
    outw_ref,
    grad_ref,
    sum_value_ref,
    sum_out_ref,
    out_full,
    pair_rows,
    rest_rows,
    pair_out,
    layer_rows,
    part,
    parts_in,
    cross,
    heads,
    head_away,
    turned,
    line,
    backs,
    mixed,
    delta_low,
    delta_mid,
    above,
    below,
    other,
    out_parts,
    value_parts,
    out_in,
    value_in,
    out_pre,
    value_pre,
    out_core,
    value_core,
    pair_out_s,
    pair_out_r,
    turned_s,
    turned_r,
    head_s,
    head_r,
    mixed_s,
    mixed_r,
    backs_s,
    backs_r,
    layer_s,
    layer_r,
    outw_s,
    outw_r,
    outw_relay,
    value_s,
    value_r,
    value_relay,
    near_s,
    near_r,
    near_relay,
    part_s,
    part_r,
    cross_s,
    cross_r,
    cross_relay,
    line_s,
    line_r,
    wave_s,
    wave_r,
    grad_s,
    grad_r,
    vcore_s,
    vcore_r,
    vsum_s,
    vsum_r,
    ocore_s,
    ocore_r,
    osum_s,
    osum_r,
):
    section = lax.axis_index("section")
    me = lax.axis_index("dp")
    z, side = section // 2, section % 2
    away = 1 - side
    half_dp = n_dp // 2
    my_half, my_place = me // half_dp, me % half_dp
    n_chip = n_dp // 2
    chip, core = me // 2, me % 2
    sibling = {"dp": me + 1 - 2 * core}
    rows, head = value_ref.shape
    half = rows * half_dp
    chunk_count = half // chunk
    seq = heads.shape[0]
    lower = {"section": lax.rem(z + n_z - 1, n_z) * 2 + side}
    upper = {"section": lax.rem(z + 1, n_z) * 2 + side}
    partner = {"section": z * 2 + away}
    own_lanes = pl.ds(pl.multiple_of(side * head, head), head)
    away_lanes = pl.ds(pl.multiple_of(away * head, head), head)
    own_seq = pl.ds(pl.multiple_of(side * seq, seq), seq)
    away_seq = pl.ds(pl.multiple_of(away * seq, seq), seq)

    def peer(step):
        return lax.rem(me + 2 * step, n_dp)

    def shard(place):
        return pl.ds(pl.multiple_of(place * rows, 16), rows)

    def remote(src, dst, send, recv, device):
        return pltpu.make_async_remote_copy(
            src_ref=src, dst_ref=dst, send_sem=send, recv_sem=recv, device_id=device, device_id_type=MESH
        )

    barrier = pltpu.get_barrier_semaphore()
    for device in (lower, upper):
        pl.semaphore_signal(barrier, inc=1, device_id=device, device_id_type=MESH)

    def greet(step, carry):
        for target in (0, 1):
            @pl.when((target != side) | (step > 0))
            def _():
                pl.semaphore_signal(
                    barrier, inc=1, device_id={"section": z * 2 + target, "dp": lax.rem(me + step, n_dp)}, device_id_type=MESH
                )
        return carry

    lax.fori_loop(0, n_dp, greet, 0)
    pl.semaphore_wait(barrier, 2 * n_dp + 1)

    pair_copy = remote(outw_ref, pair_out.at[:, own_lanes], pair_out_s, pair_out_r, partner)
    pair_copy.start()

    def layer_copy(slot, src):
        return remote(src, layer_rows.at[slot], layer_s.at[slot], layer_r.at[slot], lower)

    @pl.when(z > 0)
    def _():
        layer_copy(z, value_ref).start()

    def each_step(first, do):
        def body(step, carry):
            do(step)
            return carry

        lax.fori_loop(first, n_chip, body, 0)

    def beside(step):
        return {"dp": jnp.where(step == 0, me + 1 - 2 * core, peer(step))}

    def outw_copy(step):
        return remote(outw_ref, out_full.at[shard(me)], outw_s.at[step], outw_r.at[me], beside(step))

    def value_spot(source, do):
        place = shard(lax.rem(source, half_dp))

        @pl.when(source // half_dp == side)
        def _():
            do(pair_rows.at[place, own_lanes])

        @pl.when(source // half_dp != side)
        def _():
            do(rest_rows.at[place])

    def value_copy(step, spot):
        return remote(value_ref, spot, value_s.at[step], value_r.at[me], beside(step))

    def near_copy(step):
        return remote(
            value_ref,
            pair_rows.at[shard(my_place), own_lanes],
            near_s.at[step],
            near_r.at[my_place],
            {"section": z * 2 + away, "dp": peer(step)},
        )

    each_step(0, lambda step: outw_copy(step).start())
    turned_copy = remote(turned_ref.at[away], turned.at[side], turned_s, turned_r, partner)
    turned_copy.start()
    value_spot(me, lambda spot: each_step(0, lambda step: value_copy(step, spot).start()))

    @pl.when(my_half == away)
    def _():
        each_step(0, lambda step: near_copy(step).start())

    turned[side] = turned_ref[side]
    out_full[shard(me)] = outw_ref[...]
    pair_out[:, own_lanes] = outw_ref[...]
    layer_rows[z] = value_ref[...]

    @pl.when(my_half == side)
    def _():
        pair_rows[shard(my_place), own_lanes] = value_ref[...]

    @pl.when(my_half != side)
    def _():
        rest_rows[shard(my_place)] = value_ref[...]

    remote(outw_ref, pair_out.at[:, away_lanes], pair_out_s, pair_out_r, partner).wait_recv()

    def part_copy(slot):
        return remote(part.at[slot], parts_in.at[me], part_s.at[slot], part_r.at[me], {"dp": slot})

    def cross_block(slot, target):
        return cross.at[slot, pl.ds(pl.multiple_of(target * head, head), head)]

    def cross_copy(step, target):
        spare = (step == 0) & (target == side)
        device = {"section": z * 2 + target, "dp": jnp.where(spare, me + 1 - 2 * core, peer(step))}
        block = cross_block(me, side)
        return remote(block, block, cross_s.at[target * n_chip + step], cross_r.at[2 * me + side], device)

    def sum_parts():
        def add(step, total):
            source = lax.rem(me + step, n_dp)
            remote(part.at[0], parts_in.at[source], part_s.at[0], part_r.at[source], {"dp": source}).wait_recv()
            return total + parts_in[source].astype(F32)

        total = lax.fori_loop(1, n_dp, add, part[me].astype(F32))
        cross[me, own_lanes] = total.astype(BF16)
        for target in (0, 1):
            each_step(0, lambda step: cross_copy(step, target).start())

    def cross_part(slot, carry):
        @pl.when(slot > z)
        def _():
            layer_copy(slot, layer_rows.at[slot]).wait_recv()

            @pl.when(z > 0)
            def _():
                layer_copy(slot, layer_rows.at[slot]).start()

        part[slot] = dot_rows(layer_rows[slot], pair_out[...]).astype(BF16)

        @pl.when(me != slot)
        def _():
            part_copy(slot).start()

        return carry

    lax.fori_loop(z, n_z, cross_part, 0)

    def outw_wait(source):
        remote(outw_ref, out_full.at[shard(source)], outw_s.at[0], outw_r.at[source], sibling).wait_recv()

    def outw_on(step):
        rows_in = out_full.at[shard(peer(step))]
        return remote(rows_in, rows_in, outw_relay.at[step], outw_r.at[peer(step)], sibling)

    def outw_pass(step):
        outw_wait(peer(step))
        outw_on(step).start()

    each_step(1, outw_pass)

    @pl.when((me >= z) & (me < n_z))
    def _():
        sum_parts()

    each_step(0, lambda step: outw_wait(2 * step + 1 - core))
    own_heads = dot(cot_ref[...], out_full[...])
    backs_f32 = jnp.where(side == 0, own_heads[:seq], own_heads[seq:])
    heads[:, own_lanes] = backs_f32
    head_away[...] = jnp.where(side == 0, own_heads[seq:], own_heads[:seq])
    head_copy = remote(head_away, heads.at[:, own_lanes], head_s, head_r, partner)
    head_copy.start()
    remote(head_away, heads.at[:, away_lanes], head_s, head_r, partner).wait_recv()
    remote(turned_ref.at[side], turned.at[away], turned_s, turned_r, partner).wait_recv()

    def line_copy(slot):
        return remote(line.at[slot], line.at[slot], line_s.at[slot], line_r.at[slot], lower)

    def cross_on(slot, target):
        block = cross_block(slot, target)
        return remote(block, block, cross_relay.at[slot // 2 * 2 + target], cross_r.at[2 * slot + target], sibling)

    def each_cross_on(do):
        def at(slot, carry):
            for target in (0, 1):
                @pl.when((slot % 2 == core) & ((slot != me) | (target != side)))
                def _():
                    do(slot, target)

            return carry

        lax.fori_loop(z, n_z, at, 0)

    def cross_pass(slot, target):
        cross_on(slot, target).wait_recv()
        cross_on(slot, target).start()

    each_cross_on(cross_pass)

    def cross_wait(slot):
        @pl.when(slot % 2 != core)
        def _():
            for target in (0, 1):
                cross_on(slot, target).wait_recv()

    def take(i, total):
        slot = n_z - 1 - i
        line_copy(slot).wait_recv()

        @pl.when(z > 0)
        def _():
            line_copy(slot).start()

        cross_wait(slot)
        return total + dot(line[slot], cross[slot])

    total = lax.fori_loop(0, n_z - 1 - z, take, heads[...])
    back_top = dot(turned[1, :, :seq], total[:, head:].astype(BF16)).astype(BF16)
    cross_wait(z)
    low_head = total[:, :head] + dot(back_top, cross[z, head:, :head])
    back_low = dot(turned[0, :, :seq], low_head.astype(BF16)).astype(BF16)
    line[z, :, :head] = back_low
    line[z, :, head:] = back_top

    @pl.when(z > 0)
    def _():
        line_copy(z).start()

    backs[own_seq, :head] = back_low
    backs[own_seq, head:] = back_top
    backs_copy = remote(line.at[z], backs.at[own_seq], backs_s, backs_r, partner)
    backs_copy.start()
    remote(line.at[z], backs.at[away_seq], backs_s, backs_r, partner).wait_recv()

    def value_on(step, spot):
        return remote(spot, spot, value_relay.at[step], value_r.at[peer(step)], sibling)

    def value_pass(step):
        def do(spot):
            value_on(step, spot).wait_recv()
            value_on(step, spot).start()

        value_spot(peer(step), do)

    def value_wait(step):
        source = 2 * step + 1 - core
        value_spot(
            source, lambda spot: remote(spot, spot, value_s.at[0], value_r.at[source], sibling).wait_recv()
        )

    def near_on(i, parity):
        place = 2 * i + parity
        spot = pair_rows.at[shard(place), away_lanes]
        return remote(spot, spot, near_relay.at[i], near_r.at[place], sibling)

    each_step(1, value_pass)
    for i in range(half_dp // 2):
        near_on(i, core).wait_recv()
        near_on(i, core).start()
    each_step(0, value_wait)
    for i in range(half_dp // 2):
        near_on(i, 1 - core).wait_recv()

    for k in range(chunk_count):
        weights = pair_rows[pl.ds(k * chunk, chunk), :]
        delta_low[k] = dot_lanes(backs[...], weights)
        delta_mid[k] = dot_lanes(backs[:, head:], weights[:, head:])

    def half_lanes(which):
        return pl.ds(pl.multiple_of(which * half, 128), half)

    projected = (
        dot(acts_ref[:, half_lanes(side)], pair_rows[:, own_lanes]) + dot(acts_ref[:, half_lanes(away)], rest_rows[...])
    ).astype(BF16)
    mixed[side, :seq] = dot_rows(turned_ref[0, :, :seq], projected[:seq]).astype(BF16)
    mixed[side, seq:] = dot_rows(turned_ref[1, :, :seq], projected[seq:]).astype(BF16)
    mixed_copy = remote(mixed.at[side], mixed.at[side], mixed_s, mixed_r, partner)
    mixed_copy.start()

    def vcore_copy(i):
        return remote(
            value_parts.at[shard(2 * i + 1 - core)], value_core.at[i], vcore_s.at[i], vcore_r.at[i], sibling
        )

    def vsum_copy(step):
        to = peer(step)
        return remote(value_pre.at[to // 2], value_in.at[chip], vsum_s.at[step], vsum_r.at[chip], {"dp": to})

    def value_gradient():
        own_back = backs[:, own_lanes]
        for k in range(2 * chunk_count):
            value_parts[pl.ds(k * chunk, chunk)] = dot_rows(acts_ref[:, pl.ds(k * chunk, chunk)], own_back).astype(BF16)
        each_step(0, lambda i: vcore_copy(i).start())

    def value_send():
        def at(step):
            to = peer(step)
            vcore_copy(to // 2).wait_recv()
            value_pre[to // 2] = (value_parts[shard(to)].astype(F32) + value_core[to // 2].astype(F32)).astype(BF16)

            @pl.when(step > 0)
            def _():
                vsum_copy(step).start()

        each_step(0, at)

    @pl.when(z < n_z - 1)
    def _():
        value_gradient()

    remote(mixed.at[side], mixed.at[away], mixed_s, mixed_r, partner).wait_recv()

    @pl.when(z < n_z - 1)
    def _():
        value_send()

    def wave_copy(k):
        return remote(below.at[k], above.at[k], wave_s.at[k], wave_r.at[k], lower)

    def columns(which, k):
        return pl.ds(pl.multiple_of(which * half + k * chunk, 128), chunk)

    def grad_copy(k):
        return remote(other.at[k], grad_ref.at[:, columns(side, k)], grad_s.at[k], grad_r.at[k], partner)

    def ocore_copy(layer, i):
        at = layer * (half_dp // 2) + i // 2
        return remote(
            out_parts.at[layer, pl.ds(i * rows, rows)], out_core.at[at], ocore_s.at[at], ocore_r.at[at], sibling
        )

    def osum_copy(layer, i):
        at = layer * (half_dp // 2) + i // 2
        device = {"section": z * 2 + layer, "dp": side * half_dp + i}
        return remote(out_pre.at[at], out_in.at[chip], osum_s.at[at], osum_r.at[chip], device)

    def is_own(layer, i):
        return (layer == side) & (side * half_dp + i == me)

    def out_share(i):
        @pl.when(i % 2 != core)
        def _():
            for layer in (0, 1):
                ocore_copy(layer, i).start()

    def out_send(i):
        @pl.when(i % 2 == core)
        def _():
            for layer in (0, 1):
                at = layer * (half_dp // 2) + i // 2
                ocore_copy(layer, i).wait_recv()
                out_pre[at] = (
                    out_parts[layer, pl.ds(i * rows, rows)].astype(F32) + out_core[at].astype(F32)
                ).astype(BF16)

                @pl.when(jnp.logical_not(is_own(layer, i)))
                def _():
                    osum_copy(layer, i).start()

                @pl.when(is_own(layer, i))
                def _():
                    out_in[chip] = out_pre[at]

    shared, sent = 0, 0
    for k in range(chunk_count):
        @pl.when(z == n_z - 1)
        def _():
            above[k] = cot_ref[:, columns(side, k)]

        @pl.when(z < n_z - 1)
        def _():
            wave_copy(k).wait_recv()

        taken = above[k]
        low = (taken.astype(F32) + delta_low[k]).astype(BF16)
        below[k] = low

        @pl.when(z > 0)
        def _():
            wave_copy(k).start()

        mid = (taken.astype(F32) + delta_mid[k]).astype(BF16)
        grad_ref[:, columns(side, k)] = jnp.where(side == 1, mid, low)
        other[k] = jnp.where(side == 1, low, mid)
        grad_copy(k).start()
        out_parts[0, pl.ds(k * chunk, chunk)] = dot_rows(mid, mixed[0]).astype(BF16)
        out_parts[1, pl.ds(k * chunk, chunk)] = dot_rows(taken, mixed[1]).astype(BF16)
        while sent < shared:
            out_send(sent)
            sent += 1
        while (shared + 1) * rows <= (k + 1) * chunk:
            out_share(shared)
            shared += 1
    while sent < shared:
        out_send(sent)
        sent += 1

    @pl.when(z == n_z - 1)
    def _():
        value_gradient()
        value_send()

    total = value_pre[chip].astype(F32)
    for step in range(1, n_chip):
        source = peer(step) // 2
        remote(value_pre.at[0], value_in.at[source], vsum_s.at[step], vsum_r.at[source], sibling).wait_recv()
        total = total + value_in[source].astype(F32)
    sum_value_ref[...] = total

    total = jnp.zeros((rows, head), F32)
    for source in range(n_chip):
        @pl.when((my_half != side) | (source != chip))
        def _():
            remote(out_pre.at[0], out_in.at[source], osum_s.at[0], osum_r.at[source], sibling).wait_recv()

        total = total + out_in[source].astype(F32)
    sum_out_ref[...] = total

    for k in range(chunk_count):
        grad_copy(k).wait_send()
        remote(other.at[k], grad_ref.at[:, columns(away, k)], grad_s.at[k], grad_r.at[k], partner).wait_recv()

    pair_copy.wait_send()
    turned_copy.wait_send()
    head_copy.wait_send()
    backs_copy.wait_send()
    mixed_copy.wait_send()
    each_step(0, lambda step: outw_copy(step).wait_send())
    each_step(1, lambda step: outw_on(step).wait_send())
    value_spot(me, lambda spot: each_step(0, lambda step: value_copy(step, spot).wait_send()))
    each_step(1, lambda step: value_spot(peer(step), lambda spot: value_on(step, spot).wait_send()))

    @pl.when(my_half == away)
    def _():
        each_step(0, lambda step: near_copy(step).wait_send())

    for i in range(half_dp // 2):
        near_on(i, core).wait_send()
    each_step(0, lambda i: vcore_copy(i).wait_send())
    each_step(1, lambda step: vsum_copy(step).wait_send())
    each_cross_on(lambda slot, target: cross_on(slot, target).wait_send())

    def part_sent(slot, carry):
        @pl.when(me != slot)
        def _():
            part_copy(slot).wait_send()

        return carry

    lax.fori_loop(z, n_z, part_sent, 0)

    @pl.when((me >= z) & (me < n_z))
    def _():
        for target in (0, 1):
            each_step(0, lambda step: cross_copy(step, target).wait_send())

    for layer in (0, 1):
        for i in range(half_dp):
            @pl.when(i % 2 != core)
            def _():
                ocore_copy(layer, i).wait_send()

            @pl.when((i % 2 == core) & jnp.logical_not(is_own(layer, i)))
            def _():
                osum_copy(layer, i).wait_send()

    @pl.when(z > 0)
    def _():
        layer_copy(z, value_ref).wait_send()

        def layer_sent(slot, carry):
            layer_copy(slot, layer_rows.at[slot]).wait_send()
            return carry

        lax.fori_loop(z + 1, n_z, layer_sent, 0)

        def line_sent(slot, carry):
            line_copy(slot).wait_send()
            return carry

        lax.fori_loop(z, n_z, line_sent, 0)
        for k in range(chunk_count):
            wave_copy(k).wait_send()


def shards(acts, scores, segments, cotangent, w_value, w_out):
    n_dp = lax.axis_size("dp")
    n_z = lax.axis_size("section") // 2
    tokens = acts[0]
    row_count, feat_width = tokens.shape
    seq_len = segments.shape[1]
    shard_rows, head = w_value.shape[1:]
    half = feat_width // 2
    chunk = 256 if half % 256 == 0 else 128
    chunks = half // chunk

    probs = masked_probs(scores[0], segments)
    turned = jnp.pad(jnp.swapaxes(probs, 1, 2), ((0, 0), (0, 0), (0, 128 - seq_len)))

    vmem = pl.BlockSpec(memory_space=pltpu.VMEM)
    dma = pltpu.SemaphoreType.DMA
    one, per_z, per_dp, per_chunk, per_chip = dma, dma((n_z,)), dma((n_dp,)), dma((chunks,)), dma((n_dp // 2,))
    grad_input, grad_value, grad_out = pl.pallas_call(
        functools.partial(kernel, n_z, n_dp, chunk),
        out_shape=(
            jax.ShapeDtypeStruct((row_count, feat_width), BF16),
            jax.ShapeDtypeStruct((shard_rows, head), F32),
            jax.ShapeDtypeStruct((shard_rows, head), F32),
        ),
        in_specs=[vmem] * 5,
        out_specs=(vmem,) * 3,
        scratch_shapes=[
            pltpu.VMEM((feat_width, head), BF16),
            pltpu.VMEM((half, 2 * head), BF16),
            pltpu.VMEM((half, head), BF16),
            pltpu.VMEM((shard_rows, 2 * head), BF16),
            pltpu.VMEM((n_z, shard_rows, head), BF16),
            pltpu.VMEM((n_z, head, 2 * head), BF16),
            pltpu.VMEM((n_dp, head, 2 * head), BF16),
            pltpu.VMEM((n_z, 2 * head, 2 * head), BF16),
            pltpu.VMEM((seq_len, 2 * head), F32),
            pltpu.VMEM((seq_len, head), F32),
            pltpu.VMEM((2, seq_len, 128), BF16),
            pltpu.VMEM((n_z, seq_len, 2 * head), BF16),
            pltpu.VMEM((row_count, 2 * head), BF16),
            pltpu.VMEM((2, row_count, head), BF16),
            pltpu.VMEM((chunks, row_count, chunk), F32),
            pltpu.VMEM((chunks, row_count, chunk), F32),
            pltpu.VMEM((chunks, row_count, chunk), BF16),
            pltpu.VMEM((chunks, row_count, chunk), BF16),
            pltpu.VMEM((chunks, row_count, chunk), BF16),
            pltpu.VMEM((2, half, head), BF16),
            pltpu.VMEM((feat_width, head), BF16),
            pltpu.VMEM((n_dp // 2, shard_rows, head), BF16),
            pltpu.VMEM((n_dp // 2, shard_rows, head), BF16),
            pltpu.VMEM((n_dp // 2, shard_rows, head), BF16),
            pltpu.VMEM((n_dp // 2, shard_rows, head), BF16),
            pltpu.VMEM((n_dp // 2, shard_rows, head), BF16),
            pltpu.VMEM((n_dp // 2, shard_rows, head), BF16),
            *([one] * 10),
            per_z,
            per_z,
            per_chip,
            per_dp,
            per_chip,
            per_chip,
            per_dp,
            per_chip,
            per_chip,
            per_chip,
            per_chip,
            per_z,
            per_dp,
            per_dp,
            dma((2 * n_z,)),
            per_z,
            per_z,
            per_z,
            per_chunk,
            per_chunk,
            per_chunk,
            per_chunk,
            per_chip,
            per_chip,
            per_chip,
            per_chip,
            per_chip,
            per_chip,
            per_chip,
            per_chip,
        ],
        compiler_params=pltpu.CompilerParams(
            collective_id=0, has_side_effects=True, vmem_limit_bytes=52 << 20
        ),
        name="backward",
    )(tokens, cotangent, turned, w_value[0], w_out[0])
    return (grad_input[None], grad_value[None], grad_out[None])


def solution(mesh):
    placed = (
        P("section", "dp", None),
        P("section", "dp", None, None),
        P("dp", None),
        P("dp", None),
        P("section", "dp", None),
        P("section", "dp", None),
    )
    return jax.shard_map(
        shards,
        mesh=mesh,
        in_specs=placed,
        out_specs=(P("section", "dp", None), P("section", "dp", None), P("section", "dp", None)),
        check_vma=False,
    )
```

```python
import functools

import jax
import jax.numpy as jnp
from jax import lax
from jax.experimental import pallas as pl
from jax.experimental.pallas import tpu as pltpu
from jax.sharding import PartitionSpec as P

MESH = pl.DeviceIdType.MESH
F32 = jnp.float32
BF16 = jnp.bfloat16


def masked_probs(logits, doc_ids):
    seq_len = logits.shape[-1]
    places = jnp.arange(seq_len)
    allowed = (places[None, :, None] >= places[None, None, :]) & (
        doc_ids[:, :, None] == doc_ids[:, None, :]
    )
    kept = jnp.where(allowed, logits, -jnp.inf)
    row_top = jnp.max(kept, axis=-1, keepdims=True)
    expo = jnp.where(allowed, jnp.exp(kept - row_top), jnp.zeros_like(logits))
    return (expo / jnp.sum(expo, axis=-1, keepdims=True)).astype(BF16)


def dot(a, b):
    return jnp.dot(a, b, preferred_element_type=F32)


def dot_rows(a, b):
    return lax.dot_general(a, b, (((0,), (0,)), ((), ())), preferred_element_type=F32)


def dot_lanes(a, b):
    return lax.dot_general(a, b, (((1,), (1,)), ((), ())), preferred_element_type=F32)


def kernel(
    n_z,
    n_dp,
    chunk,
    acts_ref,
    cot_ref,
    turned_ref,
    value_ref,
    outw_ref,
    grad_ref,
    sum_value_ref,
    sum_out_ref,
    out_full,
    pair_rows,
    rest_rows,
    pair_out,
    layer_rows,
    part,
    parts_in,
    cross,
    heads,
    head_away,
    ahead,
    newest,
    turned,
    line,
    backs,
    mixed,
    delta_low,
    delta_mid,
    above,
    below,
    other,
    out_parts,
    value_parts,
    out_in,
    value_in,
    out_pre,
    value_pre,
    out_core,
    value_core,
    pair_out_s,
    pair_out_r,
    turned_s,
    turned_r,
    head_s,
    head_r,
    mixed_s,
    mixed_r,
    backs_s,
    backs_r,
    layer_s,
    layer_r,
    climb_s,
    outw_s,
    outw_r,
    outw_relay,
    value_s,
    value_r,
    value_relay,
    near_s,
    near_r,
    near_relay,
    part_s,
    part_r,
    cross_s,
    cross_r,
    cross_relay,
    line_s,
    line_r,
    next_s,
    wave_s,
    wave_r,
    grad_s,
    grad_r,
    vcore_s,
    vcore_r,
    vsum_s,
    vsum_r,
    ocore_s,
    ocore_r,
    osum_s,
    osum_r,
):
    section = lax.axis_index("section")
    me = lax.axis_index("dp")
    z, side = section // 2, section % 2
    away = 1 - side
    half_dp = n_dp // 2
    my_half, my_place = me // half_dp, me % half_dp
    n_chip = n_dp // 2
    chip, core = me // 2, me % 2
    sibling = {"dp": me + 1 - 2 * core}

    n_y = n_dp // 4

    def summer(slot):
        turn = n_z - 1 - slot
        y = lax.rem(turn, n_y)
        return 4 * y + 2 * lax.rem(y + turn // n_y, 2) + lax.rem(turn // (2 * n_y), 2)

    my_slot = n_z - 1 - (me // 4 + n_y * (lax.rem(me // 2 + me // 4, 2) + 2 * core))
    rows, head = value_ref.shape
    half = rows * half_dp
    chunk_count = half // chunk
    seq = heads.shape[0]
    lower = {"section": lax.rem(z + n_z - 1, n_z) * 2 + side}
    upper = {"section": lax.rem(z + 1, n_z) * 2 + side}
    lower_two = {"section": lax.rem(z + n_z - 2, n_z) * 2 + side}
    upper_two = {"section": lax.rem(z + 2, n_z) * 2 + side}
    partner = {"section": z * 2 + away}
    own_lanes = pl.ds(pl.multiple_of(side * head, head), head)
    away_lanes = pl.ds(pl.multiple_of(away * head, head), head)
    own_seq = pl.ds(pl.multiple_of(side * seq, seq), seq)
    away_seq = pl.ds(pl.multiple_of(away * seq, seq), seq)

    def peer(step):
        return lax.rem(me + 2 * step, n_dp)

    def shard(place):
        return pl.ds(pl.multiple_of(place * rows, 16), rows)

    def remote(src, dst, send, recv, device):
        return pltpu.make_async_remote_copy(
            src_ref=src, dst_ref=dst, send_sem=send, recv_sem=recv, device_id=device, device_id_type=MESH
        )

    barrier = pltpu.get_barrier_semaphore()
    for device in (lower, upper, lower_two, upper_two):
        pl.semaphore_signal(barrier, inc=1, device_id=device, device_id_type=MESH)

    def greet(step, carry):
        for target in (0, 1):
            @pl.when((target != side) | (step > 0))
            def _():
                pl.semaphore_signal(
                    barrier, inc=1, device_id={"section": z * 2 + target, "dp": lax.rem(me + step, n_dp)}, device_id_type=MESH
                )
        return carry

    lax.fori_loop(0, n_dp, greet, 0)
    reach = n_z // 2

    @pl.when(z == 0)
    def _():
        for above_z in range(reach + 1, n_z):
            pl.semaphore_signal(barrier, inc=1, device_id={"section": above_z * 2 + side}, device_id_type=MESH)

    pl.semaphore_wait(barrier, 2 * n_dp + 3 + jnp.where(z > reach, 1, 0))

    pair_copy = remote(outw_ref, pair_out.at[:, own_lanes], pair_out_s, pair_out_r, partner)
    pair_copy.start()

    def layer_copy(slot, src):
        return remote(src, layer_rows.at[slot], layer_s.at[slot], layer_r.at[slot], lower)

    def climb_copy(slot, src):
        return remote(src, layer_rows.at[slot], climb_s.at[slot], layer_r.at[slot], upper)

    def top_copy():
        return remote(value_ref, layer_rows.at[z], climb_s.at[z], layer_r.at[z], {"section": side})

    @pl.when(z > 0)
    def _():
        layer_copy(z, value_ref).start()

    @pl.when(z > reach)
    def _():
        top_copy().start()

    def each_step(first, do):
        def body(step, carry):
            do(step)
            return carry

        lax.fori_loop(first, n_chip, body, 0)

    def beside(step):
        return {"dp": jnp.where(step == 0, me + 1 - 2 * core, peer(step))}

    def outw_copy(step):
        return remote(outw_ref, out_full.at[shard(me)], outw_s.at[step], outw_r.at[me], beside(step))

    def value_spot(source, do):
        place = shard(lax.rem(source, half_dp))

        @pl.when(source // half_dp == side)
        def _():
            do(pair_rows.at[place, own_lanes])

        @pl.when(source // half_dp != side)
        def _():
            do(rest_rows.at[place])

    def value_copy(step, spot):
        return remote(value_ref, spot, value_s.at[step], value_r.at[me], beside(step))

    def near_copy(step):
        return remote(
            value_ref,
            pair_rows.at[shard(my_place), own_lanes],
            near_s.at[step],
            near_r.at[my_place],
            {"section": z * 2 + away, "dp": peer(step)},
        )

    each_step(0, lambda step: outw_copy(step).start())
    turned_copy = remote(turned_ref.at[away], turned.at[side], turned_s, turned_r, partner)
    turned_copy.start()

    def value_start():
        value_spot(me, lambda spot: each_step(0, lambda step: value_copy(step, spot).start()))

        @pl.when(my_half == away)
        def _():
            each_step(0, lambda step: near_copy(step).start())

    late = n_z - n_z // 4

    @pl.when(z < late)
    def _():
        value_start()

    turned[side] = turned_ref[side]
    out_full[shard(me)] = outw_ref[...]
    pair_out[:, own_lanes] = outw_ref[...]
    layer_rows[z] = value_ref[...]

    @pl.when(my_half == side)
    def _():
        pair_rows[shard(my_place), own_lanes] = value_ref[...]

    @pl.when(my_half != side)
    def _():
        rest_rows[shard(my_place)] = value_ref[...]

    remote(outw_ref, pair_out.at[:, away_lanes], pair_out_s, pair_out_r, partner).wait_recv()

    def part_copy(slot):
        return remote(part.at[slot], parts_in.at[me], part_s.at[slot], part_r.at[me], {"dp": summer(slot)})

    def cross_block(slot, target):
        return cross.at[slot, pl.ds(pl.multiple_of(target * head, head), head)]

    def cross_copy(step, target):
        spare = (step == 0) & (target == side)
        device = {"section": z * 2 + target, "dp": jnp.where(spare, me + 1 - 2 * core, peer(step))}
        block = cross_block(my_slot, side)
        return remote(block, block, cross_s.at[target * n_chip + step], cross_r.at[2 * my_slot + side], device)

    def sum_parts():
        def add(step, total):
            source = lax.rem(me + step, n_dp)
            remote(part.at[0], parts_in.at[source], part_s.at[0], part_r.at[source], {"dp": source}).wait_recv()
            return total + parts_in[source].astype(F32)

        total = lax.fori_loop(1, n_dp, add, part[my_slot].astype(F32))
        cross[my_slot, own_lanes] = total.astype(BF16)
        for target in (0, 1):
            each_step(0, lambda step: cross_copy(step, target).start())

    def cross_part(slot):
        part[slot] = dot_rows(layer_rows[slot], pair_out[...]).astype(BF16)

        @pl.when(slot != my_slot)
        def _():
            part_copy(slot).start()

    def goes_down(k):
        return (z > 0) & (z + k < n_z) & (k < reach)

    def climbing(k):
        here = (k < reach) & (k > z)
        return lax.rem(z - k + n_z, n_z), here, here & (k + 1 < reach)

    def gather_step(k, carry):
        slot, here, onward = climbing(k)

        @pl.when(z + k < n_z)
        def _():
            layer_copy(z + k, layer_rows.at[z + k]).wait_recv()

        @pl.when(goes_down(k))
        def _():
            layer_copy(z + k, layer_rows.at[z + k]).start()

        @pl.when(here)
        def _():
            climb_copy(slot, layer_rows.at[slot]).wait_recv()

        @pl.when(onward)
        def _():
            climb_copy(slot, layer_rows.at[slot]).start()

        @pl.when(z + k < n_z)
        def _():
            cross_part(z + k)

        @pl.when(here)
        def _():
            cross_part(slot)

        return carry

    cross_part(z)
    lax.fori_loop(1, reach + 1, gather_step, 0)

    def outw_wait(source):
        remote(outw_ref, out_full.at[shard(source)], outw_s.at[0], outw_r.at[source], sibling).wait_recv()

    def outw_on(step):
        rows_in = out_full.at[shard(peer(step))]
        return remote(rows_in, rows_in, outw_relay.at[step], outw_r.at[peer(step)], sibling)

    def outw_pass(step):
        outw_wait(peer(step))
        outw_on(step).start()

    each_step(1, outw_pass)

    each_step(0, lambda step: outw_wait(2 * step + 1 - core))
    own_heads = dot(cot_ref[...], out_full[...])
    backs_f32 = jnp.where(side == 0, own_heads[:seq], own_heads[seq:])
    heads[:, own_lanes] = backs_f32
    head_away[...] = jnp.where(side == 0, own_heads[seq:], own_heads[:seq])
    head_copy = remote(head_away, heads.at[:, own_lanes], head_s, head_r, partner)
    head_copy.start()

    @pl.when(my_slot >= z)
    def _():
        sum_parts()

    @pl.when(z >= late)
    def _():
        value_start()

    remote(head_away, heads.at[:, away_lanes], head_s, head_r, partner).wait_recv()
    remote(turned_ref.at[side], turned.at[away], turned_s, turned_r, partner).wait_recv()

    def line_copy(slot):
        return remote(line.at[slot], line.at[slot], line_s.at[slot], line_r.at[slot], lower_two)

    def next_copy():
        return remote(line.at[z], line.at[z], next_s, line_r.at[z], lower)

    def cross_on(slot, target):
        block = cross_block(slot, target)
        return remote(block, block, cross_relay.at[2 * slot + target], cross_r.at[2 * slot + target], sibling)

    def each_cross_on(do):
        def at(slot, carry):
            for target in (0, 1):
                @pl.when((summer(slot) % 2 == core) & ((slot != my_slot) | (target != side)))
                def _():
                    do(slot, target)

            return carry

        lax.fori_loop(z, n_z, at, 0)

    def cross_pass(slot, target):
        cross_on(slot, target).wait_recv()
        cross_on(slot, target).start()

    each_cross_on(cross_pass)

    def value_on(step, spot):
        return remote(spot, spot, value_relay.at[step], value_r.at[peer(step)], sibling)

    def value_pass(step):
        def do(spot):
            value_on(step, spot).wait_recv()
            value_on(step, spot).start()

        value_spot(peer(step), do)

    def value_wait(step):
        source = 2 * step + 1 - core
        value_spot(
            source, lambda spot: remote(spot, spot, value_s.at[0], value_r.at[source], sibling).wait_recv()
        )

    def near_on(i, parity):
        place = 2 * i + parity
        spot = pair_rows.at[shard(place), away_lanes]
        return remote(spot, spot, near_relay.at[i], near_r.at[place], sibling)

    def half_lanes(which):
        return pl.ds(pl.multiple_of(which * half, 128), half)

    mixed_copy = remote(mixed.at[side], mixed.at[side], mixed_s, mixed_r, partner)

    def mix():
        each_step(1, value_pass)
        for i in range(half_dp // 2):
            near_on(i, core).wait_recv()
            near_on(i, core).start()
        each_step(0, value_wait)
        for i in range(half_dp // 2):
            near_on(i, 1 - core).wait_recv()
        projected = (
            dot(acts_ref[:, half_lanes(side)], pair_rows[:, own_lanes]) + dot(acts_ref[:, half_lanes(away)], rest_rows[...])
        ).astype(BF16)
        mixed[side, :seq] = dot_rows(turned_ref[0, :, :seq], projected[:seq]).astype(BF16)
        mixed[side, seq:] = dot_rows(turned_ref[1, :, :seq], projected[seq:]).astype(BF16)
        mixed_copy.start()

    early = n_z // 2 - 2

    @pl.when(z < early)
    def _():
        mix()

    def mix_late():
        @pl.when(z >= early)
        def _():
            mix()

    def cross_wait(slot):
        @pl.when(summer(slot) % 2 != core)
        def _():
            for target in (0, 1):
                cross_on(slot, target).wait_recv()

    def line_on(slot):
        @pl.when(z > 1)
        def _():
            line_copy(slot).start()

    def take(i, total):
        slot = n_z - 1 - i
        line_copy(slot).wait_recv()
        line_on(slot)
        cross_wait(slot)
        return total + dot(line[slot], cross[slot])

    cross_wait(z)
    inner = cross[z, head:, :head]
    twice = dot(turned[0, :, :seq], turned[1, :, :seq]).astype(BF16)
    low_turned = jnp.concatenate([turned[0, :, :seq], twice], axis=1)

    @pl.when(z < n_z - 1)
    def _():
        cross_wait(z + 1)
        ahead[:, : 2 * head] = cross[z + 1]
        ahead[:, 2 * head :] = dot(cross[z + 1, :, head:], inner).astype(BF16)

    total = lax.fori_loop(0, n_z - 2 - z, take, heads[...])
    crossed = dot(total[:, head:].astype(BF16), inner)

    @pl.when(z == n_z - 1)
    def _():
        newest[...] = jnp.zeros_like(newest)

    @pl.when(z < n_z - 1)
    def _():
        line_copy(z + 1).wait_recv()
        newest[...] = dot(line[z + 1], ahead[...])

    low_head = (total[:, :head] + newest[:, :head]).astype(BF16)
    top_head = (total[:, head:] + newest[:, head : 2 * head]).astype(BF16)
    crossed = (crossed + newest[:, 2 * head :]).astype(BF16)
    back_top = dot(turned[1, :, :seq], top_head).astype(BF16)
    back_low = dot(low_turned, jnp.concatenate([low_head, crossed], axis=0)).astype(BF16)
    line[z, :, :head] = back_low
    line[z, :, head:] = back_top

    @pl.when(z > 0)
    def _():
        next_copy().start()

    backs[own_seq, :head] = back_low
    backs[own_seq, head:] = back_top
    backs_copy = remote(line.at[z], backs.at[own_seq], backs_s, backs_r, partner)
    backs_copy.start()

    @pl.when(z > 0)
    def _():
        next_copy().wait_send()

    line_on(z)

    @pl.when(z < n_z - 1)
    def _():
        line_on(z + 1)

    remote(line.at[z], backs.at[away_seq], backs_s, backs_r, partner).wait_recv()

    mix_late()
    for k in range(chunk_count):
        weights = pair_rows[pl.ds(k * chunk, chunk), :]
        delta_low[k] = dot_lanes(backs[...], weights)
        delta_mid[k] = dot_lanes(backs[:, head:], weights[:, head:])

    def vcore_copy(i):
        return remote(
            value_parts.at[shard(2 * i + 1 - core)], value_core.at[i], vcore_s.at[i], vcore_r.at[i], sibling
        )

    def vsum_copy(step):
        to = peer(step)
        return remote(value_pre.at[to // 2], value_in.at[chip], vsum_s.at[step], vsum_r.at[chip], {"dp": to})

    def value_gradient():
        own_back = backs[:, own_lanes]
        for k in range(2 * chunk_count):
            value_parts[pl.ds(k * chunk, chunk)] = dot_rows(acts_ref[:, pl.ds(k * chunk, chunk)], own_back).astype(BF16)
        each_step(0, lambda i: vcore_copy(i).start())

    def value_send():
        def at(step):
            to = peer(step)
            vcore_copy(to // 2).wait_recv()
            value_pre[to // 2] = (value_parts[shard(to)].astype(F32) + value_core[to // 2].astype(F32)).astype(BF16)

            @pl.when(step > 0)
            def _():
                vsum_copy(step).start()

        each_step(0, at)

    @pl.when(z < n_z - 1)
    def _():
        value_gradient()

    remote(mixed.at[side], mixed.at[away], mixed_s, mixed_r, partner).wait_recv()

    def wave_copy(k):
        return remote(below.at[k], above.at[k], wave_s.at[k], wave_r.at[k], lower)

    def columns(which, k):
        return pl.ds(pl.multiple_of(which * half + k * chunk, 128), chunk)

    def grad_copy(k):
        return remote(other.at[k], grad_ref.at[:, columns(side, k)], grad_s.at[k], grad_r.at[k], partner)

    def ocore_copy(layer, i):
        at = layer * (half_dp // 2) + i // 2
        return remote(
            out_parts.at[layer, pl.ds(i * rows, rows)], out_core.at[at], ocore_s.at[at], ocore_r.at[at], sibling
        )

    def osum_copy(layer, i):
        at = layer * (half_dp // 2) + i // 2
        device = {"section": z * 2 + layer, "dp": side * half_dp + i}
        return remote(out_pre.at[at], out_in.at[chip], osum_s.at[at], osum_r.at[chip], device)

    def is_own(layer, i):
        return (layer == side) & (side * half_dp + i == me)

    def out_share(i):
        @pl.when(i % 2 != core)
        def _():
            for layer in (0, 1):
                ocore_copy(layer, i).start()

    def out_send(i):
        @pl.when(i % 2 == core)
        def _():
            for layer in (0, 1):
                at = layer * (half_dp // 2) + i // 2
                ocore_copy(layer, i).wait_recv()
                out_pre[at] = (
                    out_parts[layer, pl.ds(i * rows, rows)].astype(F32) + out_core[at].astype(F32)
                ).astype(BF16)

                @pl.when(jnp.logical_not(is_own(layer, i)))
                def _():
                    osum_copy(layer, i).start()

                @pl.when(is_own(layer, i))
                def _():
                    out_in[chip] = out_pre[at]

    shared, sent = 0, 0
    for k in range(chunk_count):
        if k == min(3, chunk_count - 1):

            @pl.when(z < n_z - 1)
            def _():
                value_send()

        @pl.when(z == n_z - 1)
        def _():
            above[k] = cot_ref[:, columns(side, k)]

        @pl.when(z < n_z - 1)
        def _():
            wave_copy(k).wait_recv()

        taken = above[k]
        low = (taken.astype(F32) + delta_low[k]).astype(BF16)
        below[k] = low

        @pl.when(z > 0)
        def _():
            wave_copy(k).start()

        mid = (taken.astype(F32) + delta_mid[k]).astype(BF16)
        grad_ref[:, columns(side, k)] = jnp.where(side == 1, mid, low)
        other[k] = jnp.where(side == 1, low, mid)
        grad_copy(k).start()
        out_parts[0, pl.ds(k * chunk, chunk)] = dot_rows(mid, mixed[0]).astype(BF16)
        out_parts[1, pl.ds(k * chunk, chunk)] = dot_rows(taken, mixed[1]).astype(BF16)
        while sent < shared:
            out_send(sent)
            sent += 1
        while (shared + 1) * rows <= (k + 1) * chunk:
            out_share(shared)
            shared += 1
    while sent < shared:
        out_send(sent)
        sent += 1

    @pl.when(z == n_z - 1)
    def _():
        value_gradient()
        value_send()

    total = value_pre[chip].astype(F32)
    for step in range(1, n_chip):
        source = peer(step) // 2
        remote(value_pre.at[0], value_in.at[source], vsum_s.at[step], vsum_r.at[source], sibling).wait_recv()
        total = total + value_in[source].astype(F32)
    sum_value_ref[...] = total

    total = jnp.zeros((rows, head), F32)
    for source in range(n_chip):
        @pl.when((my_half != side) | (source != chip))
        def _():
            remote(out_pre.at[0], out_in.at[source], osum_s.at[0], osum_r.at[source], sibling).wait_recv()

        total = total + out_in[source].astype(F32)
    sum_out_ref[...] = total

    for k in range(chunk_count):
        grad_copy(k).wait_send()
        remote(other.at[k], grad_ref.at[:, columns(away, k)], grad_s.at[k], grad_r.at[k], partner).wait_recv()

    pair_copy.wait_send()
    turned_copy.wait_send()
    head_copy.wait_send()
    backs_copy.wait_send()
    mixed_copy.wait_send()
    each_step(0, lambda step: outw_copy(step).wait_send())
    each_step(1, lambda step: outw_on(step).wait_send())
    value_spot(me, lambda spot: each_step(0, lambda step: value_copy(step, spot).wait_send()))
    each_step(1, lambda step: value_spot(peer(step), lambda spot: value_on(step, spot).wait_send()))

    @pl.when(my_half == away)
    def _():
        each_step(0, lambda step: near_copy(step).wait_send())

    for i in range(half_dp // 2):
        near_on(i, core).wait_send()
    each_step(0, lambda i: vcore_copy(i).wait_send())
    each_step(1, lambda step: vsum_copy(step).wait_send())
    each_cross_on(lambda slot, target: cross_on(slot, target).wait_send())

    def part_sent(slot, carry):
        @pl.when(slot != my_slot)
        def _():
            part_copy(slot).wait_send()

        return carry

    lax.fori_loop(z, n_z, part_sent, 0)

    @pl.when(my_slot >= z)
    def _():
        for target in (0, 1):
            each_step(0, lambda step: cross_copy(step, target).wait_send())

    for layer in (0, 1):
        for i in range(half_dp):
            @pl.when(i % 2 != core)
            def _():
                ocore_copy(layer, i).wait_send()

            @pl.when((i % 2 == core) & jnp.logical_not(is_own(layer, i)))
            def _():
                osum_copy(layer, i).wait_send()

    @pl.when(z > reach)
    def _():
        top_copy().wait_send()

    def gather_sent(k, carry):
        slot, here, onward = climbing(k)

        @pl.when(goes_down(k))
        def _():
            layer_copy(z + k, layer_rows.at[z + k]).wait_send()

        @pl.when(onward)
        def _():
            climb_copy(slot, layer_rows.at[slot]).wait_send()

        return carry

    lax.fori_loop(1, reach + 1, gather_sent, 0)

    @pl.when(z > 0)
    def _():
        layer_copy(z, value_ref).wait_send()
        for k in range(chunk_count):
            wave_copy(k).wait_send()

    @pl.when(z > 1)
    def _():
        def line_sent(slot, carry):
            line_copy(slot).wait_send()
            return carry

        lax.fori_loop(z, n_z, line_sent, 0)


def shards(acts, scores, segments, cotangent, w_value, w_out):
    n_dp = lax.axis_size("dp")
    n_z = lax.axis_size("section") // 2
    tokens = acts[0]
    row_count, feat_width = tokens.shape
    seq_len = segments.shape[1]
    shard_rows, head = w_value.shape[1:]
    half = feat_width // 2
    chunk = 256 if half % 256 == 0 else 128
    chunks = half // chunk

    probs = masked_probs(scores[0], segments)
    turned = jnp.pad(jnp.swapaxes(probs, 1, 2), ((0, 0), (0, 0), (0, 128 - seq_len)))

    vmem = pl.BlockSpec(memory_space=pltpu.VMEM)
    dma = pltpu.SemaphoreType.DMA
    one, per_z, per_dp, per_chunk, per_chip = dma, dma((n_z,)), dma((n_dp,)), dma((chunks,)), dma((n_dp // 2,))
    grad_input, grad_value, grad_out = pl.pallas_call(
        functools.partial(kernel, n_z, n_dp, chunk),
        out_shape=(
            jax.ShapeDtypeStruct((row_count, feat_width), BF16),
            jax.ShapeDtypeStruct((shard_rows, head), F32),
            jax.ShapeDtypeStruct((shard_rows, head), F32),
        ),
        in_specs=[vmem] * 5,
        out_specs=(vmem,) * 3,
        scratch_shapes=[
            pltpu.VMEM((feat_width, head), BF16),
            pltpu.VMEM((half, 2 * head), BF16),
            pltpu.VMEM((half, head), BF16),
            pltpu.VMEM((shard_rows, 2 * head), BF16),
            pltpu.VMEM((n_z, shard_rows, head), BF16),
            pltpu.VMEM((n_z, head, 2 * head), BF16),
            pltpu.VMEM((n_dp, head, 2 * head), BF16),
            pltpu.VMEM((n_z, 2 * head, 2 * head), BF16),
            pltpu.VMEM((seq_len, 2 * head), F32),
            pltpu.VMEM((seq_len, head), F32),
            pltpu.VMEM((2 * head, 3 * head), BF16),
            pltpu.VMEM((seq_len, 3 * head), F32),
            pltpu.VMEM((2, seq_len, 128), BF16),
            pltpu.VMEM((n_z, seq_len, 2 * head), BF16),
            pltpu.VMEM((row_count, 2 * head), BF16),
            pltpu.VMEM((2, row_count, head), BF16),
            pltpu.VMEM((chunks, row_count, chunk), F32),
            pltpu.VMEM((chunks, row_count, chunk), F32),
            pltpu.VMEM((chunks, row_count, chunk), BF16),
            pltpu.VMEM((chunks, row_count, chunk), BF16),
            pltpu.VMEM((chunks, row_count, chunk), BF16),
            pltpu.VMEM((2, half, head), BF16),
            pltpu.VMEM((feat_width, head), BF16),
            pltpu.VMEM((n_dp // 2, shard_rows, head), BF16),
            pltpu.VMEM((n_dp // 2, shard_rows, head), BF16),
            pltpu.VMEM((n_dp // 2, shard_rows, head), BF16),
            pltpu.VMEM((n_dp // 2, shard_rows, head), BF16),
            pltpu.VMEM((n_dp // 2, shard_rows, head), BF16),
            pltpu.VMEM((n_dp // 2, shard_rows, head), BF16),
            *([one] * 10),
            per_z,
            per_z,
            per_z,
            per_chip,
            per_dp,
            per_chip,
            per_chip,
            per_dp,
            per_chip,
            per_chip,
            per_chip,
            per_chip,
            per_z,
            per_dp,
            per_dp,
            dma((2 * n_z,)),
            dma((2 * n_z,)),
            per_z,
            per_z,
            one,
            per_chunk,
            per_chunk,
            per_chunk,
            per_chunk,
            per_chip,
            per_chip,
            per_chip,
            per_chip,
            per_chip,
            per_chip,
            per_chip,
            per_chip,
        ],
        compiler_params=pltpu.CompilerParams(
            collective_id=0, has_side_effects=True, vmem_limit_bytes=52 << 20
        ),
        name="backward",
    )(tokens, cotangent, turned, w_value[0], w_out[0])
    return (grad_input[None], grad_value[None], grad_out[None])


def solution(mesh):
    placed = (
        P("section", "dp", None),
        P("section", "dp", None, None),
        P("dp", None),
        P("dp", None),
        P("section", "dp", None),
        P("section", "dp", None),
    )
    return jax.shard_map(
        shards,
        mesh=mesh,
        in_specs=placed,
        out_specs=(P("section", "dp", None), P("section", "dp", None), P("section", "dp", None)),
        check_vma=False,
    )
```

```python
import functools

import jax
import jax.numpy as jnp
from jax import lax
from jax.experimental import pallas as pl
from jax.experimental.pallas import tpu as pltpu
from jax.sharding import PartitionSpec as P

MESH = pl.DeviceIdType.MESH
F32 = jnp.float32
BF16 = jnp.bfloat16


def masked_probs(logits, doc_ids):
    seq_len = logits.shape[-1]
    places = jnp.arange(seq_len)
    allowed = (places[None, :, None] >= places[None, None, :]) & (
        doc_ids[:, :, None] == doc_ids[:, None, :]
    )
    kept = jnp.where(allowed, logits, -jnp.inf)
    row_top = jnp.max(kept, axis=-1, keepdims=True)
    expo = jnp.where(allowed, jnp.exp(kept - row_top), jnp.zeros_like(logits))
    return (expo / jnp.sum(expo, axis=-1, keepdims=True)).astype(BF16)


def dot(a, b):
    return jnp.dot(a, b, preferred_element_type=F32)


def dot_rows(a, b):
    return lax.dot_general(a, b, (((0,), (0,)), ((), ())), preferred_element_type=F32)


def dot_lanes(a, b):
    return lax.dot_general(a, b, (((1,), (1,)), ((), ())), preferred_element_type=F32)


def kernel(
    n_z,
    n_dp,
    chunk,
    acts_ref,
    cot_ref,
    turned_ref,
    value_ref,
    outw_ref,
    grad_ref,
    sum_value_ref,
    sum_out_ref,
    out_full,
    pair_rows,
    rest_rows,
    pair_out,
    layer_rows,
    part,
    parts_in,
    cross,
    heads,
    head_away,
    ahead,
    newest,
    turned,
    line,
    backs,
    mixed,
    delta_low,
    delta_mid,
    above,
    below,
    middle,
    other,
    out_parts,
    value_parts,
    out_in,
    value_in,
    out_pre,
    value_pre,
    out_core,
    value_core,
    pair_out_s,
    pair_out_r,
    turned_s,
    turned_r,
    head_s,
    head_r,
    mixed_s,
    mixed_r,
    backs_s,
    backs_r,
    layer_s,
    layer_r,
    climb_s,
    outw_s,
    outw_r,
    outw_relay,
    value_s,
    value_r,
    value_relay,
    near_s,
    near_r,
    near_relay,
    part_s,
    part_r,
    cross_s,
    cross_r,
    cross_relay,
    line_s,
    line_r,
    wave_s,
    wave_r,
    grad_s,
    grad_r,
    vcore_s,
    vcore_r,
    vsum_s,
    vsum_r,
    ocore_s,
    ocore_r,
    osum_s,
    osum_r,
):
    section = lax.axis_index("section")
    me = lax.axis_index("dp")
    z, side = section // 2, section % 2
    away = 1 - side
    half_dp = n_dp // 2
    my_half, my_place = me // half_dp, me % half_dp
    n_chip = n_dp // 2
    chip, core = me // 2, me % 2
    sibling = {"dp": me + 1 - 2 * core}

    n_y = n_dp // 4

    def summer(slot):
        turn = n_z - 1 - slot
        y = lax.rem(turn, n_y)
        return 4 * y + 2 * lax.rem(y + turn // n_y, 2) + lax.rem(turn // (2 * n_y), 2)

    my_slot = n_z - 1 - (me // 4 + n_y * (lax.rem(me // 2 + me // 4, 2) + 2 * core))
    rows, head = value_ref.shape
    half = rows * half_dp
    chunk_count = half // chunk
    seq = heads.shape[0]
    lower = {"section": lax.rem(z + n_z - 1, n_z) * 2 + side}
    upper = {"section": lax.rem(z + 1, n_z) * 2 + side}
    partner = {"section": z * 2 + away}
    own_lanes = pl.ds(pl.multiple_of(side * head, head), head)
    away_lanes = pl.ds(pl.multiple_of(away * head, head), head)
    own_seq = pl.ds(pl.multiple_of(side * seq, seq), seq)
    away_seq = pl.ds(pl.multiple_of(away * seq, seq), seq)

    def peer(step):
        return lax.rem(me + 2 * step, n_dp)

    def shard(place):
        return pl.ds(pl.multiple_of(place * rows, 16), rows)

    def remote(src, dst, send, recv, device):
        return pltpu.make_async_remote_copy(
            src_ref=src, dst_ref=dst, send_sem=send, recv_sem=recv, device_id=device, device_id_type=MESH
        )

    barrier = pltpu.get_barrier_semaphore()
    for device in (lower, upper):
        pl.semaphore_signal(barrier, inc=1, device_id=device, device_id_type=MESH)

    def greet(step, carry):
        for target in (0, 1):
            @pl.when((target != side) | (step > 0))
            def _():
                pl.semaphore_signal(
                    barrier, inc=1, device_id={"section": z * 2 + target, "dp": lax.rem(me + step, n_dp)}, device_id_type=MESH
                )
        return carry

    lax.fori_loop(0, n_dp, greet, 0)
    reach = n_z // 2

    @pl.when(z == 0)
    def _():
        for above_z in range(reach + 1, n_z):
            pl.semaphore_signal(barrier, inc=1, device_id={"section": above_z * 2 + side}, device_id_type=MESH)

    pl.semaphore_wait(barrier, 2 * n_dp + 1 + jnp.where(z > reach, 1, 0))

    pair_copy = remote(outw_ref, pair_out.at[:, own_lanes], pair_out_s, pair_out_r, partner)
    pair_copy.start()

    part_rows = rows // 2

    def rows_of(ref, piece):
        return ref.at[pl.ds(piece * part_rows, part_rows)]

    def stream(slot, src, sems, device):
        return [
            remote(
                rows_of(src, piece),
                rows_of(layer_rows.at[slot], piece),
                sems.at[2 * slot + piece],
                layer_r.at[2 * slot + piece],
                device,
            )
            for piece in (0, 1)
        ]

    def layer_copies(slot, src):
        return stream(slot, src, layer_s, lower)

    def climb_copies(slot, src):
        return stream(slot, src, climb_s, upper)

    def top_copies():
        return stream(z, value_ref, climb_s, {"section": side})

    @pl.when(z > 0)
    def _():
        for copy in layer_copies(z, value_ref):
            copy.start()

    @pl.when(z > reach)
    def _():
        for copy in top_copies():
            copy.start()

    def each_step(first, do):
        def body(step, carry):
            do(step)
            return carry

        lax.fori_loop(first, n_chip, body, 0)

    def beside(step):
        return {"dp": jnp.where(step == 0, me + 1 - 2 * core, peer(step))}

    def outw_copy(step):
        return remote(outw_ref, out_full.at[shard(me)], outw_s.at[step], outw_r.at[me], beside(step))

    def value_spot(source, do):
        place = shard(lax.rem(source, half_dp))

        @pl.when(source // half_dp == side)
        def _():
            do(pair_rows.at[place, own_lanes])

        @pl.when(source // half_dp != side)
        def _():
            do(rest_rows.at[place])

    def value_copy(step, spot):
        return remote(value_ref, spot, value_s.at[step], value_r.at[me], beside(step))

    def near_copy(step):
        return remote(
            value_ref,
            pair_rows.at[shard(my_place), own_lanes],
            near_s.at[step],
            near_r.at[my_place],
            {"section": z * 2 + away, "dp": peer(step)},
        )

    each_step(0, lambda step: outw_copy(step).start())
    turned_copy = remote(turned_ref.at[away], turned.at[side], turned_s, turned_r, partner)
    turned_copy.start()

    def value_start():
        value_spot(me, lambda spot: each_step(0, lambda step: value_copy(step, spot).start()))

        @pl.when(my_half == away)
        def _():
            each_step(0, lambda step: near_copy(step).start())

    late = n_z - n_z // 4

    @pl.when(z < late)
    def _():
        value_start()

    turned[side] = turned_ref[side]
    out_full[shard(me)] = outw_ref[...]
    pair_out[:, own_lanes] = outw_ref[...]
    layer_rows[z] = value_ref[...]

    @pl.when(my_half == side)
    def _():
        pair_rows[shard(my_place), own_lanes] = value_ref[...]

    @pl.when(my_half != side)
    def _():
        rest_rows[shard(my_place)] = value_ref[...]

    remote(outw_ref, pair_out.at[:, away_lanes], pair_out_s, pair_out_r, partner).wait_recv()

    def used(slot, target):
        return (slot > z) | (target == 1)

    sums_here = (my_slot >= z) & used(my_slot, side)

    def part_copy(slot):
        return remote(part.at[slot], parts_in.at[me], part_s.at[slot], part_r.at[me], {"dp": summer(slot)})

    def cross_block(slot, target):
        return cross.at[slot, pl.ds(pl.multiple_of(target * head, head), head)]

    def cross_copy(step, target):
        spare = (step == 0) & (target == side)
        device = {"section": z * 2 + target, "dp": jnp.where(spare, me + 1 - 2 * core, peer(step))}
        block = cross_block(my_slot, side)
        return remote(block, block, cross_s.at[target * n_chip + step], cross_r.at[2 * my_slot + side], device)

    def sum_parts():
        def add(step, total):
            source = lax.rem(me + step, n_dp)
            remote(part.at[0], parts_in.at[source], part_s.at[0], part_r.at[source], {"dp": source}).wait_recv()
            return total + parts_in[source].astype(F32)

        total = lax.fori_loop(1, n_dp, add, part[my_slot].astype(F32))
        cross[my_slot, own_lanes] = total.astype(BF16)
        for target in (0, 1):
            each_step(0, lambda step: cross_copy(step, target).start())

    def cross_part(slot):
        part[slot] = dot_rows(layer_rows[slot], pair_out[...]).astype(BF16)

        @pl.when((slot != my_slot) & used(slot, side))
        def _():
            part_copy(slot).start()

    def goes_down(k):
        return (z > 0) & (z + k < n_z) & (k < reach)

    def climbing(k):
        here = (k < reach) & (k > z)
        return lax.rem(z - k + n_z, n_z), here, here & (k + 1 < reach)

    def gather_step(k, carry):
        slot, here, onward = climbing(k)

        @pl.when(z + k < n_z)
        def _():
            for copy in layer_copies(z + k, layer_rows.at[z + k]):
                copy.wait_recv()

                @pl.when(goes_down(k))
                def _():
                    copy.start()

        @pl.when(here)
        def _():
            for copy in climb_copies(slot, layer_rows.at[slot]):
                copy.wait_recv()

                @pl.when(onward)
                def _():
                    copy.start()

        @pl.when(z + k < n_z)
        def _():
            cross_part(z + k)

        @pl.when(here)
        def _():
            cross_part(slot)

        return carry

    cross_part(z)
    lax.fori_loop(1, reach + 1, gather_step, 0)

    @pl.when(sums_here & (z >= late))
    def _():
        sum_parts()

    def outw_wait(source):
        remote(outw_ref, out_full.at[shard(source)], outw_s.at[0], outw_r.at[source], sibling).wait_recv()

    def outw_on(step):
        rows_in = out_full.at[shard(peer(step))]
        return remote(rows_in, rows_in, outw_relay.at[step], outw_r.at[peer(step)], sibling)

    def outw_pass(step):
        outw_wait(peer(step))
        outw_on(step).start()

    each_step(1, outw_pass)

    each_step(0, lambda step: outw_wait(2 * step + 1 - core))
    own_heads = dot(cot_ref[...], out_full[...])
    backs_f32 = jnp.where(side == 0, own_heads[:seq], own_heads[seq:])
    heads[:, own_lanes] = backs_f32
    head_away[...] = jnp.where(side == 0, own_heads[seq:], own_heads[:seq])
    head_copy = remote(head_away, heads.at[:, own_lanes], head_s, head_r, partner)
    head_copy.start()

    @pl.when(sums_here & (z < late))
    def _():
        sum_parts()

    @pl.when(z >= late)
    def _():
        value_start()


    def line_copy(slot):
        return remote(line.at[slot], line.at[slot], line_s.at[slot], line_r.at[slot], lower)

    def cross_on(slot, target):
        block = cross_block(slot, target)
        return remote(block, block, cross_relay.at[2 * slot + target], cross_r.at[2 * slot + target], sibling)

    def each_cross_on(do):
        def at(slot, carry):
            for target in (0, 1):
                @pl.when((summer(slot) % 2 == core) & ((slot != my_slot) | (target != side)) & used(slot, target))
                def _():
                    do(slot, target)

            return carry

        lax.fori_loop(z, n_z, at, 0)

    def cross_pass(slot, target):
        cross_on(slot, target).wait_recv()
        cross_on(slot, target).start()

    def value_on(step, spot):
        return remote(spot, spot, value_relay.at[step], value_r.at[peer(step)], sibling)

    def value_pass(step):
        def do(spot):
            value_on(step, spot).wait_recv()
            value_on(step, spot).start()

        value_spot(peer(step), do)

    def value_wait(step):
        source = 2 * step + 1 - core
        value_spot(
            source, lambda spot: remote(spot, spot, value_s.at[0], value_r.at[source], sibling).wait_recv()
        )

    def near_on(i, parity):
        place = 2 * i + parity
        spot = pair_rows.at[shard(place), away_lanes]
        return remote(spot, spot, near_relay.at[i], near_r.at[place], sibling)

    def half_lanes(which):
        return pl.ds(pl.multiple_of(which * half, 128), half)

    mixed_copy = remote(mixed.at[side], mixed.at[side], mixed_s, mixed_r, partner)

    def mix_relay():
        each_step(1, value_pass)
        for i in range(half_dp // 2):
            near_on(i, core).wait_recv()
            near_on(i, core).start()

    def mix():
        each_step(0, value_wait)
        for i in range(half_dp // 2):
            near_on(i, 1 - core).wait_recv()
        projected = (
            dot(acts_ref[:, half_lanes(side)], pair_rows[:, own_lanes]) + dot(acts_ref[:, half_lanes(away)], rest_rows[...])
        ).astype(BF16)
        mixed[side, :seq] = dot_rows(turned_ref[0, :, :seq], projected[:seq]).astype(BF16)
        mixed[side, seq:] = dot_rows(turned_ref[1, :, :seq], projected[seq:]).astype(BF16)
        mixed_copy.start()

    early = n_z // 2 - 2

    @pl.when(z < early)
    def _():
        mix_relay()

    each_cross_on(cross_pass)

    @pl.when(z < early)
    def _():
        mix()

    def mix_late():
        @pl.when(z >= early)
        def _():
            mix_relay()
            mix()

    def cross_wait(slot):
        for target in (0, 1):
            @pl.when((summer(slot) % 2 != core) & used(slot, target))
            def _():
                cross_on(slot, target).wait_recv()

    def line_on(slot):
        @pl.when(z > 0)
        def _():
            line_copy(slot).start()

    def take(i, total):
        slot = n_z - 1 - i
        line_copy(slot).wait_recv()
        line_on(slot)
        cross_wait(slot)
        return total + dot(line[slot], cross[slot])

    remote(head_away, heads.at[:, away_lanes], head_s, head_r, partner).wait_recv()
    remote(turned_ref.at[side], turned.at[away], turned_s, turned_r, partner).wait_recv()
    cross_wait(z)
    inner = cross[z, head:, :head]
    twice = dot(turned[0, :, :seq], turned[1, :, :seq]).astype(BF16)
    low_turned = jnp.concatenate([turned[0, :, :seq], twice], axis=1)

    @pl.when(z < n_z - 1)
    def _():
        cross_wait(z + 1)
        ahead[:, : 2 * head] = cross[z + 1]
        ahead[:, 2 * head :] = dot(cross[z + 1, :, head:], inner).astype(BF16)

    total = lax.fori_loop(0, n_z - 2 - z, take, heads[...])
    crossed = dot(total[:, head:].astype(BF16), inner)

    @pl.when(z == n_z - 1)
    def _():
        newest[...] = jnp.zeros_like(newest)

    @pl.when(z < n_z - 1)
    def _():
        line_copy(z + 1).wait_recv()
        line_on(z + 1)
        newest[...] = dot(line[z + 1], ahead[...])

    low_head = (total[:, :head] + newest[:, :head]).astype(BF16)
    top_head = (total[:, head:] + newest[:, head : 2 * head]).astype(BF16)
    crossed = (crossed + newest[:, 2 * head :]).astype(BF16)
    back_top = dot(turned[1, :, :seq], top_head).astype(BF16)
    back_low = dot(low_turned, jnp.concatenate([low_head, crossed], axis=0)).astype(BF16)
    line[z, :, :head] = back_low
    line[z, :, head:] = back_top

    line_on(z)
    backs[own_seq, :head] = back_low
    backs[own_seq, head:] = back_top
    backs_copy = remote(line.at[z], backs.at[own_seq], backs_s, backs_r, partner)
    backs_copy.start()

    remote(line.at[z], backs.at[away_seq], backs_s, backs_r, partner).wait_recv()

    mix_late()
    for k in range(chunk_count):
        weights = pair_rows[pl.ds(k * chunk, chunk), :]
        delta_low[k] = dot_lanes(backs[...], weights)
        delta_mid[k] = dot_lanes(backs[:, head:], weights[:, head:])

    def vcore_copy(i):
        return remote(
            value_parts.at[shard(2 * i + 1 - core)], value_core.at[i], vcore_s.at[i], vcore_r.at[i], sibling
        )

    def vsum_copy(step):
        to = peer(step)
        return remote(value_pre.at[to // 2], value_in.at[chip], vsum_s.at[step], vsum_r.at[chip], {"dp": to})

    def value_gradient():
        own_back = backs[:, own_lanes]
        for k in range(2 * chunk_count):
            value_parts[pl.ds(k * chunk, chunk)] = dot_rows(acts_ref[:, pl.ds(k * chunk, chunk)], own_back).astype(BF16)
        each_step(0, lambda i: vcore_copy(i).start())

    def value_send(step):
        to = peer(step)
        vcore_copy(to // 2).wait_recv()
        value_pre[to // 2] = (value_parts[shard(to)].astype(F32) + value_core[to // 2].astype(F32)).astype(BF16)
        if step > 0:
            vsum_copy(step).start()

    @pl.when(z < n_z - 1)
    def _():
        value_gradient()

    def wave_copy(k):
        return remote(below.at[k], above.at[k], wave_s.at[k], wave_r.at[k], lower)

    def columns(which, k):
        return pl.ds(pl.multiple_of(which * half + k * chunk, 128), chunk)

    def grad_copy(k):
        return remote(other.at[k], grad_ref.at[:, columns(side, k)], grad_s.at[k], grad_r.at[k], partner)

    def ocore_copy(layer, i):
        at = layer * (half_dp // 2) + i // 2
        return remote(
            out_parts.at[layer, pl.ds(i * rows, rows)], out_core.at[at], ocore_s.at[at], ocore_r.at[at], sibling
        )

    def osum_copy(layer, i):
        at = layer * (half_dp // 2) + i // 2
        device = {"section": z * 2 + layer, "dp": side * half_dp + i}
        return remote(out_pre.at[at], out_in.at[chip], osum_s.at[at], osum_r.at[chip], device)

    def is_own(layer, i):
        return (layer == side) & (side * half_dp + i == me)

    def out_share(i):
        @pl.when(i % 2 != core)
        def _():
            for layer in (0, 1):
                ocore_copy(layer, i).start()

    def out_send(i):
        @pl.when(i % 2 == core)
        def _():
            for layer in (0, 1):
                at = layer * (half_dp // 2) + i // 2
                ocore_copy(layer, i).wait_recv()
                out_pre[at] = (
                    out_parts[layer, pl.ds(i * rows, rows)].astype(F32) + out_core[at].astype(F32)
                ).astype(BF16)

                @pl.when(jnp.logical_not(is_own(layer, i)))
                def _():
                    osum_copy(layer, i).start()

                @pl.when(is_own(layer, i))
                def _():
                    out_in[chip] = out_pre[at]

    shared, sent, lag, ready = 0, 0, 2, [0, 0, 0]
    for k in range(chunk_count + lag):
        if k < chunk_count:

            @pl.when(z == n_z - 1)
            def _():
                above[k] = cot_ref[:, columns(side, k)]

            @pl.when(z < n_z - 1)
            def _():
                wave_copy(k).wait_recv()

            taken = above[k].astype(F32)
            low = (taken + delta_low[k]).astype(BF16)
            below[k] = low

            @pl.when(z > 0)
            def _():
                wave_copy(k).start()

            mid = (taken + delta_mid[k]).astype(BF16)
            middle[k] = mid
            grad_ref[:, columns(side, k)] = jnp.where(side == 1, mid, low)
            other[k] = jnp.where(side == 1, low, mid)
            grad_copy(k).start()

        if k < lag:
            continue
        if k == lag:
            remote(mixed.at[side], mixed.at[away], mixed_s, mixed_r, partner).wait_recv()

        done = k - lag
        if done < n_chip:

            @pl.when(z < n_z - 1)
            def _():
                value_send((done + 1) % n_chip)

        out_parts[0, pl.ds(done * chunk, chunk)] = dot_rows(middle[done], mixed[0]).astype(BF16)
        out_parts[1, pl.ds(done * chunk, chunk)] = dot_rows(above[done], mixed[1]).astype(BF16)
        while sent < ready[0]:
            out_send(sent)
            sent += 1
        while (shared + 1) * rows <= (done + 1) * chunk:
            out_share(shared)
            shared += 1
        ready = ready[1:] + [shared]
    while sent < shared:
        out_send(sent)
        sent += 1

    @pl.when(z == n_z - 1)
    def _():
        value_gradient()
        for step in range(n_chip):
            value_send(step)

    total = value_pre[chip].astype(F32)
    for step in range(1, n_chip):
        source = peer(step) // 2
        remote(value_pre.at[0], value_in.at[source], vsum_s.at[step], vsum_r.at[source], sibling).wait_recv()
        total = total + value_in[source].astype(F32)
    sum_value_ref[...] = total

    total = jnp.zeros((rows, head), F32)
    for source in range(n_chip):
        @pl.when((my_half != side) | (source != chip))
        def _():
            remote(out_pre.at[0], out_in.at[source], osum_s.at[0], osum_r.at[source], sibling).wait_recv()

        total = total + out_in[source].astype(F32)
    sum_out_ref[...] = total

    for k in range(chunk_count):
        grad_copy(k).wait_send()
        remote(other.at[k], grad_ref.at[:, columns(away, k)], grad_s.at[k], grad_r.at[k], partner).wait_recv()

    pair_copy.wait_send()
    turned_copy.wait_send()
    head_copy.wait_send()
    backs_copy.wait_send()
    mixed_copy.wait_send()
    each_step(0, lambda step: outw_copy(step).wait_send())
    each_step(1, lambda step: outw_on(step).wait_send())
    value_spot(me, lambda spot: each_step(0, lambda step: value_copy(step, spot).wait_send()))
    each_step(1, lambda step: value_spot(peer(step), lambda spot: value_on(step, spot).wait_send()))

    @pl.when(my_half == away)
    def _():
        each_step(0, lambda step: near_copy(step).wait_send())

    for i in range(half_dp // 2):
        near_on(i, core).wait_send()
    each_step(0, lambda i: vcore_copy(i).wait_send())
    each_step(1, lambda step: vsum_copy(step).wait_send())
    each_cross_on(lambda slot, target: cross_on(slot, target).wait_send())

    def part_sent(slot, carry):
        @pl.when((slot != my_slot) & used(slot, side))
        def _():
            part_copy(slot).wait_send()

        return carry

    lax.fori_loop(z, n_z, part_sent, 0)

    @pl.when(sums_here)
    def _():
        for target in (0, 1):
            each_step(0, lambda step: cross_copy(step, target).wait_send())

    for layer in (0, 1):
        for i in range(half_dp):
            @pl.when(i % 2 != core)
            def _():
                ocore_copy(layer, i).wait_send()

            @pl.when((i % 2 == core) & jnp.logical_not(is_own(layer, i)))
            def _():
                osum_copy(layer, i).wait_send()

    @pl.when(z > reach)
    def _():
        for copy in top_copies():
            copy.wait_send()

    def gather_sent(k, carry):
        slot, here, onward = climbing(k)

        @pl.when(goes_down(k))
        def _():
            for copy in layer_copies(z + k, layer_rows.at[z + k]):
                copy.wait_send()

        @pl.when(onward)
        def _():
            for copy in climb_copies(slot, layer_rows.at[slot]):
                copy.wait_send()

        return carry

    lax.fori_loop(1, reach + 1, gather_sent, 0)

    @pl.when(z > 0)
    def _():
        for copy in layer_copies(z, value_ref):
            copy.wait_send()
        for k in range(chunk_count):
            wave_copy(k).wait_send()

    @pl.when(z > 0)
    def _():
        def line_sent(slot, carry):
            line_copy(slot).wait_send()
            return carry

        lax.fori_loop(z, n_z, line_sent, 0)


def shards(acts, scores, segments, cotangent, w_value, w_out):
    n_dp = lax.axis_size("dp")
    n_z = lax.axis_size("section") // 2
    tokens = acts[0]
    row_count, feat_width = tokens.shape
    seq_len = segments.shape[1]
    shard_rows, head = w_value.shape[1:]
    half = feat_width // 2
    chunk = 256 if half % 256 == 0 else 128
    chunks = half // chunk

    probs = masked_probs(scores[0], segments)
    turned = jnp.pad(jnp.swapaxes(probs, 1, 2), ((0, 0), (0, 0), (0, 128 - seq_len)))

    vmem = pl.BlockSpec(memory_space=pltpu.VMEM)
    dma = pltpu.SemaphoreType.DMA
    one, per_z, per_dp, per_chunk, per_chip = dma, dma((n_z,)), dma((n_dp,)), dma((chunks,)), dma((n_dp // 2,))
    grad_input, grad_value, grad_out = pl.pallas_call(
        functools.partial(kernel, n_z, n_dp, chunk),
        out_shape=(
            jax.ShapeDtypeStruct((row_count, feat_width), BF16),
            jax.ShapeDtypeStruct((shard_rows, head), F32),
            jax.ShapeDtypeStruct((shard_rows, head), F32),
        ),
        in_specs=[vmem] * 5,
        out_specs=(vmem,) * 3,
        scratch_shapes=[
            pltpu.VMEM((feat_width, head), BF16),
            pltpu.VMEM((half, 2 * head), BF16),
            pltpu.VMEM((half, head), BF16),
            pltpu.VMEM((shard_rows, 2 * head), BF16),
            pltpu.VMEM((n_z, shard_rows, head), BF16),
            pltpu.VMEM((n_z, head, 2 * head), BF16),
            pltpu.VMEM((n_dp, head, 2 * head), BF16),
            pltpu.VMEM((n_z, 2 * head, 2 * head), BF16),
            pltpu.VMEM((seq_len, 2 * head), F32),
            pltpu.VMEM((seq_len, head), F32),
            pltpu.VMEM((2 * head, 3 * head), BF16),
            pltpu.VMEM((seq_len, 3 * head), F32),
            pltpu.VMEM((2, seq_len, 128), BF16),
            pltpu.VMEM((n_z, seq_len, 2 * head), BF16),
            pltpu.VMEM((row_count, 2 * head), BF16),
            pltpu.VMEM((2, row_count, head), BF16),
            pltpu.VMEM((chunks, row_count, chunk), F32),
            pltpu.VMEM((chunks, row_count, chunk), F32),
            pltpu.VMEM((chunks, row_count, chunk), BF16),
            pltpu.VMEM((chunks, row_count, chunk), BF16),
            pltpu.VMEM((chunks, row_count, chunk), BF16),
            pltpu.VMEM((chunks, row_count, chunk), BF16),
            pltpu.VMEM((2, half, head), BF16),
            pltpu.VMEM((feat_width, head), BF16),
            pltpu.VMEM((n_dp // 2, shard_rows, head), BF16),
            pltpu.VMEM((n_dp // 2, shard_rows, head), BF16),
            pltpu.VMEM((n_dp // 2, shard_rows, head), BF16),
            pltpu.VMEM((n_dp // 2, shard_rows, head), BF16),
            pltpu.VMEM((n_dp // 2, shard_rows, head), BF16),
            pltpu.VMEM((n_dp // 2, shard_rows, head), BF16),
            *([one] * 10),
            dma((2 * n_z,)),
            dma((2 * n_z,)),
            dma((2 * n_z,)),
            per_chip,
            per_dp,
            per_chip,
            per_chip,
            per_dp,
            per_chip,
            per_chip,
            per_chip,
            per_chip,
            per_z,
            per_dp,
            per_dp,
            dma((2 * n_z,)),
            dma((2 * n_z,)),
            per_z,
            per_z,
            per_chunk,
            per_chunk,
            per_chunk,
            per_chunk,
            per_chip,
            per_chip,
            per_chip,
            per_chip,
            per_chip,
            per_chip,
            per_chip,
            per_chip,
        ],
        compiler_params=pltpu.CompilerParams(
            collective_id=0, has_side_effects=True, vmem_limit_bytes=52 << 20
        ),
        name="backward",
    )(tokens, cotangent, turned, w_value[0], w_out[0])
    return (grad_input[None], grad_value[None], grad_out[None])


def solution(mesh):
    placed = (
        P("section", "dp", None),
        P("section", "dp", None, None),
        P("dp", None),
        P("dp", None),
        P("section", "dp", None),
        P("section", "dp", None),
    )
    return jax.shard_map(
        shards,
        mesh=mesh,
        in_specs=placed,
        out_specs=(P("section", "dp", None), P("section", "dp", None), P("section", "dp", None)),
        check_vma=False,
    )
```

```python
import functools

import jax
import jax.numpy as jnp
from jax import lax
from jax.experimental import pallas as pl
from jax.experimental.pallas import tpu as pltpu
from jax.sharding import PartitionSpec as P

MESH = pl.DeviceIdType.MESH
F32 = jnp.float32
BF16 = jnp.bfloat16


def turned_probs(scores, ids_across, ids_down):
    seq_len = scores.shape[0]
    query = lax.broadcasted_iota(jnp.int32, (seq_len, seq_len), 0)
    key = lax.broadcasted_iota(jnp.int32, (seq_len, seq_len), 1)
    allowed = (query >= key) & (ids_down == ids_across)
    kept = jnp.where(allowed, scores, -jnp.inf)
    row_top = jnp.max(kept, axis=-1, keepdims=True)
    expo = jnp.where(allowed, jnp.exp(kept - row_top), 0.0)
    return (expo / jnp.sum(expo, axis=-1, keepdims=True)).T.astype(BF16)


def dot(a, b):
    return jnp.dot(a, b, preferred_element_type=F32)


def dot_rows(a, b):
    return lax.dot_general(a, b, (((0,), (0,)), ((), ())), preferred_element_type=F32)


def dot_lanes(a, b):
    return lax.dot_general(a, b, (((1,), (1,)), ((), ())), preferred_element_type=F32)


def kernel(
    n_z,
    n_dp,
    chunk,
    acts_ref,
    cot_ref,
    scores_ref,
    across_ref,
    down_ref,
    value_ref,
    outw_ref,
    grad_ref,
    sum_value_ref,
    sum_out_ref,
    turned_ref,
    out_full,
    pair_rows,
    rest_rows,
    pair_out,
    layer_rows,
    part,
    parts_in,
    cross,
    heads,
    head_away,
    ahead,
    newest,
    turned,
    line,
    backs,
    mixed,
    delta_low,
    delta_mid,
    above,
    below,
    middle,
    other,
    out_parts,
    value_parts,
    out_in,
    value_in,
    out_pre,
    value_pre,
    out_core,
    value_core,
    pair_out_s,
    pair_out_r,
    turned_s,
    turned_r,
    head_s,
    head_r,
    mixed_s,
    mixed_r,
    backs_s,
    backs_r,
    layer_s,
    layer_r,
    climb_s,
    outw_s,
    outw_r,
    outw_relay,
    value_s,
    value_r,
    value_relay,
    near_s,
    near_r,
    near_relay,
    part_s,
    part_r,
    cross_s,
    cross_r,
    cross_relay,
    line_s,
    line_r,
    wave_s,
    wave_r,
    grad_s,
    grad_r,
    vcore_s,
    vcore_r,
    vsum_s,
    vsum_r,
    ocore_s,
    ocore_r,
    osum_s,
    osum_r,
):
    section = lax.axis_index("section")
    me = lax.axis_index("dp")
    z, side = section // 2, section % 2
    away = 1 - side
    half_dp = n_dp // 2
    my_half, my_place = me // half_dp, me % half_dp
    n_chip = n_dp // 2
    chip, core = me // 2, me % 2
    sibling = {"dp": me + 1 - 2 * core}

    n_y = n_dp // 4

    def summer(slot):
        turn = n_z - 1 - slot
        y = lax.rem(turn, n_y)
        return 4 * y + 2 * lax.rem(y + turn // n_y, 2) + lax.rem(turn // (2 * n_y), 2)

    my_slot = n_z - 1 - (me // 4 + n_y * (lax.rem(me // 2 + me // 4, 2) + 2 * core))
    rows, head = value_ref.shape
    half = rows * half_dp
    chunk_count = half // chunk
    seq = heads.shape[0]
    lower = {"section": lax.rem(z + n_z - 1, n_z) * 2 + side}
    upper = {"section": lax.rem(z + 1, n_z) * 2 + side}
    partner = {"section": z * 2 + away}
    own_lanes = pl.ds(pl.multiple_of(side * head, head), head)
    away_lanes = pl.ds(pl.multiple_of(away * head, head), head)
    own_seq = pl.ds(pl.multiple_of(side * seq, seq), seq)
    away_seq = pl.ds(pl.multiple_of(away * seq, seq), seq)

    def peer(step):
        return lax.rem(me + 2 * step, n_dp)

    def shard(place):
        return pl.ds(pl.multiple_of(place * rows, 16), rows)

    def remote(src, dst, send, recv, device):
        return pltpu.make_async_remote_copy(
            src_ref=src, dst_ref=dst, send_sem=send, recv_sem=recv, device_id=device, device_id_type=MESH
        )

    barrier = pltpu.get_barrier_semaphore()
    for device in (lower, upper):
        pl.semaphore_signal(barrier, inc=1, device_id=device, device_id_type=MESH)

    def greet(step, carry):
        for target in (0, 1):
            @pl.when((target != side) | (step > 0))
            def _():
                pl.semaphore_signal(
                    barrier, inc=1, device_id={"section": z * 2 + target, "dp": lax.rem(me + step, n_dp)}, device_id_type=MESH
                )
        return carry

    lax.fori_loop(0, n_dp, greet, 0)
    for which in (0, 1):
        turned_ref[which, :, :seq] = turned_probs(scores_ref[which], across_ref[which], down_ref[which])
        turned_ref[which, :, seq:] = jnp.zeros((seq, turned_ref.shape[2] - seq), BF16)
    reach = n_z // 2

    @pl.when(z == 0)
    def _():
        for above_z in range(reach + 1, n_z):
            pl.semaphore_signal(barrier, inc=1, device_id={"section": above_z * 2 + side}, device_id_type=MESH)

    pl.semaphore_wait(barrier, 2 * n_dp + 1 + jnp.where(z > reach, 1, 0))

    pair_copy = remote(outw_ref, pair_out.at[:, own_lanes], pair_out_s, pair_out_r, partner)
    pair_copy.start()

    part_rows = rows // 2

    def rows_of(ref, piece):
        return ref.at[pl.ds(piece * part_rows, part_rows)]

    def stream(slot, src, sems, device):
        return [
            remote(
                rows_of(src, piece),
                rows_of(layer_rows.at[slot], piece),
                sems.at[2 * slot + piece],
                layer_r.at[2 * slot + piece],
                device,
            )
            for piece in (0, 1)
        ]

    def layer_copies(slot, src):
        return stream(slot, src, layer_s, lower)

    def climb_copies(slot, src):
        return stream(slot, src, climb_s, upper)

    def top_copies():
        return stream(z, value_ref, climb_s, {"section": side})

    @pl.when(z > 0)
    def _():
        for copy in layer_copies(z, value_ref):
            copy.start()

    @pl.when(z > reach)
    def _():
        for copy in top_copies():
            copy.start()

    def each_step(first, do):
        def body(step, carry):
            do(step)
            return carry

        lax.fori_loop(first, n_chip, body, 0)

    def beside(step):
        return {"dp": jnp.where(step == 0, me + 1 - 2 * core, peer(step))}

    def outw_copy(step):
        return remote(outw_ref, out_full.at[shard(me)], outw_s.at[step], outw_r.at[me], beside(step))

    def value_spot(source, do):
        place = shard(lax.rem(source, half_dp))

        @pl.when(source // half_dp == side)
        def _():
            do(pair_rows.at[place, own_lanes])

        @pl.when(source // half_dp != side)
        def _():
            do(rest_rows.at[place])

    def value_copy(step, spot):
        return remote(value_ref, spot, value_s.at[step], value_r.at[me], beside(step))

    def near_copy(step):
        return remote(
            value_ref,
            pair_rows.at[shard(my_place), own_lanes],
            near_s.at[step],
            near_r.at[my_place],
            {"section": z * 2 + away, "dp": peer(step)},
        )

    each_step(0, lambda step: outw_copy(step).start())
    turned_copy = remote(turned_ref.at[away], turned.at[side], turned_s, turned_r, partner)
    turned_copy.start()

    def value_start():
        value_spot(me, lambda spot: each_step(0, lambda step: value_copy(step, spot).start()))

        @pl.when(my_half == away)
        def _():
            each_step(0, lambda step: near_copy(step).start())

    late = n_z - n_z // 4

    @pl.when(z < late)
    def _():
        value_start()

    turned[side] = turned_ref[side]
    out_full[shard(me)] = outw_ref[...]
    pair_out[:, own_lanes] = outw_ref[...]
    layer_rows[z] = value_ref[...]

    @pl.when(my_half == side)
    def _():
        pair_rows[shard(my_place), own_lanes] = value_ref[...]

    @pl.when(my_half != side)
    def _():
        rest_rows[shard(my_place)] = value_ref[...]

    remote(outw_ref, pair_out.at[:, away_lanes], pair_out_s, pair_out_r, partner).wait_recv()

    def used(slot, target):
        return (slot > z) | (target == 1)

    sums_here = (my_slot >= z) & used(my_slot, side)

    def part_copy(slot):
        return remote(part.at[slot], parts_in.at[me], part_s.at[slot], part_r.at[me], {"dp": summer(slot)})

    def cross_block(slot, target):
        return cross.at[slot, pl.ds(pl.multiple_of(target * head, head), head)]

    def cross_copy(step, target):
        spare = (step == 0) & (target == side)
        device = {"section": z * 2 + target, "dp": jnp.where(spare, me + 1 - 2 * core, peer(step))}
        block = cross_block(my_slot, side)
        return remote(block, block, cross_s.at[target * n_chip + step], cross_r.at[2 * my_slot + side], device)

    def sum_parts():
        def add(step, total):
            source = lax.rem(me + step, n_dp)
            remote(part.at[0], parts_in.at[source], part_s.at[0], part_r.at[source], {"dp": source}).wait_recv()
            return total + parts_in[source].astype(F32)

        total = lax.fori_loop(1, n_dp, add, part[my_slot].astype(F32))
        cross[my_slot, own_lanes] = total.astype(BF16)
        for target in (0, 1):
            each_step(0, lambda step: cross_copy(step, target).start())

    def cross_part(slot):
        part[slot] = dot_rows(layer_rows[slot], pair_out[...]).astype(BF16)

        @pl.when((slot != my_slot) & used(slot, side))
        def _():
            part_copy(slot).start()

    def goes_down(k):
        return (z > 0) & (z + k < n_z) & (k < reach)

    def climbing(k):
        here = (k < reach) & (k > z)
        return lax.rem(z - k + n_z, n_z), here, here & (k + 1 < reach)

    def gather_step(k, carry):
        slot, here, onward = climbing(k)

        @pl.when(z + k < n_z)
        def _():
            for copy in layer_copies(z + k, layer_rows.at[z + k]):
                copy.wait_recv()

                @pl.when(goes_down(k))
                def _():
                    copy.start()

        @pl.when(here)
        def _():
            for copy in climb_copies(slot, layer_rows.at[slot]):
                copy.wait_recv()

                @pl.when(onward)
                def _():
                    copy.start()

        @pl.when(z + k < n_z)
        def _():
            cross_part(z + k)

        @pl.when(here)
        def _():
            cross_part(slot)

        return carry

    cross_part(z)
    lax.fori_loop(1, reach + 1, gather_step, 0)

    @pl.when(sums_here & (z >= late))
    def _():
        sum_parts()

    def outw_wait(source):
        remote(outw_ref, out_full.at[shard(source)], outw_s.at[0], outw_r.at[source], sibling).wait_recv()

    def outw_on(step):
        rows_in = out_full.at[shard(peer(step))]
        return remote(rows_in, rows_in, outw_relay.at[step], outw_r.at[peer(step)], sibling)

    def outw_pass(step):
        outw_wait(peer(step))
        outw_on(step).start()

    each_step(1, outw_pass)

    each_step(0, lambda step: outw_wait(2 * step + 1 - core))
    own_heads = dot(cot_ref[...], out_full[...])
    backs_f32 = jnp.where(side == 0, own_heads[:seq], own_heads[seq:])
    heads[:, own_lanes] = backs_f32
    head_away[...] = jnp.where(side == 0, own_heads[seq:], own_heads[:seq])
    head_copy = remote(head_away, heads.at[:, own_lanes], head_s, head_r, partner)
    head_copy.start()

    @pl.when(sums_here & (z < late))
    def _():
        sum_parts()

    @pl.when(z >= late)
    def _():
        value_start()


    def line_copy(slot):
        return remote(line.at[slot], line.at[slot], line_s.at[slot], line_r.at[slot], lower)

    def cross_on(slot, target):
        block = cross_block(slot, target)
        return remote(block, block, cross_relay.at[2 * slot + target], cross_r.at[2 * slot + target], sibling)

    def each_cross_on(do):
        def at(slot, carry):
            for target in (0, 1):
                @pl.when((summer(slot) % 2 == core) & ((slot != my_slot) | (target != side)) & used(slot, target))
                def _():
                    do(slot, target)

            return carry

        lax.fori_loop(z, n_z, at, 0)

    def cross_pass(slot, target):
        cross_on(slot, target).wait_recv()
        cross_on(slot, target).start()

    def value_on(step, spot):
        return remote(spot, spot, value_relay.at[step], value_r.at[peer(step)], sibling)

    def value_pass(step):
        def do(spot):
            value_on(step, spot).wait_recv()
            value_on(step, spot).start()

        value_spot(peer(step), do)

    def value_wait(step):
        source = 2 * step + 1 - core
        value_spot(
            source, lambda spot: remote(spot, spot, value_s.at[0], value_r.at[source], sibling).wait_recv()
        )

    def near_on(i, parity):
        place = 2 * i + parity
        spot = pair_rows.at[shard(place), away_lanes]
        return remote(spot, spot, near_relay.at[i], near_r.at[place], sibling)

    def half_lanes(which):
        return pl.ds(pl.multiple_of(which * half, 128), half)

    mixed_copy = remote(mixed.at[side], mixed.at[side], mixed_s, mixed_r, partner)

    def mix_relay():
        each_step(1, value_pass)
        for i in range(half_dp // 2):
            near_on(i, core).wait_recv()
            near_on(i, core).start()

    def mix():
        each_step(0, value_wait)
        for i in range(half_dp // 2):
            near_on(i, 1 - core).wait_recv()
        projected = (
            dot(acts_ref[:, half_lanes(side)], pair_rows[:, own_lanes]) + dot(acts_ref[:, half_lanes(away)], rest_rows[...])
        ).astype(BF16)
        mixed[side, :seq] = dot_rows(turned_ref[0, :, :seq], projected[:seq]).astype(BF16)
        mixed[side, seq:] = dot_rows(turned_ref[1, :, :seq], projected[seq:]).astype(BF16)
        mixed_copy.start()

    early = n_z // 2 - 2

    @pl.when(z < early)
    def _():
        mix_relay()

    each_cross_on(cross_pass)

    @pl.when(z < early)
    def _():
        mix()

    def mix_late():
        @pl.when(z >= early)
        def _():
            mix_relay()
            mix()

    def cross_wait(slot):
        for target in (0, 1):
            @pl.when((summer(slot) % 2 != core) & used(slot, target))
            def _():
                cross_on(slot, target).wait_recv()

    def line_on(slot):
        @pl.when(z > 0)
        def _():
            line_copy(slot).start()

    def take(i, total):
        slot = n_z - 1 - i
        line_copy(slot).wait_recv()
        line_on(slot)
        cross_wait(slot)
        return total + dot(line[slot], cross[slot])

    remote(head_away, heads.at[:, away_lanes], head_s, head_r, partner).wait_recv()
    remote(turned_ref.at[side], turned.at[away], turned_s, turned_r, partner).wait_recv()
    cross_wait(z)
    inner = cross[z, head:, :head]
    twice = dot(turned[0, :, :seq], turned[1, :, :seq]).astype(BF16)
    low_turned = jnp.concatenate([turned[0, :, :seq], twice], axis=1)

    @pl.when(z < n_z - 1)
    def _():
        cross_wait(z + 1)
        ahead[:, : 2 * head] = cross[z + 1]
        ahead[:, 2 * head :] = dot(cross[z + 1, :, head:], inner).astype(BF16)

    total = lax.fori_loop(0, n_z - 2 - z, take, heads[...])
    crossed = dot(total[:, head:].astype(BF16), inner)

    @pl.when(z == n_z - 1)
    def _():
        newest[...] = jnp.zeros_like(newest)

    @pl.when(z < n_z - 1)
    def _():
        line_copy(z + 1).wait_recv()
        line_on(z + 1)
        newest[...] = dot(line[z + 1], ahead[...])

    low_head = (total[:, :head] + newest[:, :head]).astype(BF16)
    top_head = (total[:, head:] + newest[:, head : 2 * head]).astype(BF16)
    crossed = (crossed + newest[:, 2 * head :]).astype(BF16)
    back_top = dot(turned[1, :, :seq], top_head).astype(BF16)
    back_low = dot(low_turned, jnp.concatenate([low_head, crossed], axis=0)).astype(BF16)
    line[z, :, :head] = back_low
    line[z, :, head:] = back_top

    line_on(z)
    backs[own_seq, :head] = back_low
    backs[own_seq, head:] = back_top
    backs_copy = remote(line.at[z], backs.at[own_seq], backs_s, backs_r, partner)
    backs_copy.start()

    remote(line.at[z], backs.at[away_seq], backs_s, backs_r, partner).wait_recv()

    mix_late()
    for k in range(chunk_count):
        weights = pair_rows[pl.ds(k * chunk, chunk), :]
        delta_low[k] = dot_lanes(backs[...], weights)
        delta_mid[k] = dot_lanes(backs[:, head:], weights[:, head:])

    def vcore_copy(i):
        return remote(
            value_parts.at[shard(2 * i + 1 - core)], value_core.at[i], vcore_s.at[i], vcore_r.at[i], sibling
        )

    def vsum_copy(step):
        to = peer(step)
        return remote(value_pre.at[to // 2], value_in.at[chip], vsum_s.at[step], vsum_r.at[chip], {"dp": to})

    def value_gradient():
        own_back = backs[:, own_lanes]
        for k in range(2 * chunk_count):
            value_parts[pl.ds(k * chunk, chunk)] = dot_rows(acts_ref[:, pl.ds(k * chunk, chunk)], own_back).astype(BF16)
        each_step(0, lambda i: vcore_copy(i).start())

    def value_send(step):
        to = peer(step)
        vcore_copy(to // 2).wait_recv()
        value_pre[to // 2] = (value_parts[shard(to)].astype(F32) + value_core[to // 2].astype(F32)).astype(BF16)
        if step > 0:
            vsum_copy(step).start()

    @pl.when(z < n_z - 1)
    def _():
        value_gradient()

    def wave_copy(k):
        return remote(below.at[k], above.at[k], wave_s.at[k], wave_r.at[k], lower)

    def columns(which, k):
        return pl.ds(pl.multiple_of(which * half + k * chunk, 128), chunk)

    def grad_copy(k):
        return remote(other.at[k], grad_ref.at[:, columns(side, k)], grad_s.at[k], grad_r.at[k], partner)

    def ocore_copy(layer, i):
        at = layer * (half_dp // 2) + i // 2
        return remote(
            out_parts.at[layer, pl.ds(i * rows, rows)], out_core.at[at], ocore_s.at[at], ocore_r.at[at], sibling
        )

    def osum_copy(layer, i):
        at = layer * (half_dp // 2) + i // 2
        device = {"section": z * 2 + layer, "dp": side * half_dp + i}
        return remote(out_pre.at[at], out_in.at[chip], osum_s.at[at], osum_r.at[chip], device)

    def is_own(layer, i):
        return (layer == side) & (side * half_dp + i == me)

    def out_share(i):
        @pl.when(i % 2 != core)
        def _():
            for layer in (0, 1):
                ocore_copy(layer, i).start()

    def out_send(i):
        @pl.when(i % 2 == core)
        def _():
            for layer in (0, 1):
                at = layer * (half_dp // 2) + i // 2
                ocore_copy(layer, i).wait_recv()
                out_pre[at] = (
                    out_parts[layer, pl.ds(i * rows, rows)].astype(F32) + out_core[at].astype(F32)
                ).astype(BF16)

                @pl.when(jnp.logical_not(is_own(layer, i)))
                def _():
                    osum_copy(layer, i).start()

                @pl.when(is_own(layer, i))
                def _():
                    out_in[chip] = out_pre[at]

    shared, sent, lag, ready = 0, 0, 2, [0, 0, 0]
    for k in range(chunk_count + lag):
        if k < chunk_count:

            @pl.when(z == n_z - 1)
            def _():
                above[k] = cot_ref[:, columns(side, k)]

            @pl.when(z < n_z - 1)
            def _():
                wave_copy(k).wait_recv()

            taken = above[k].astype(F32)
            low = (taken + delta_low[k]).astype(BF16)
            below[k] = low

            @pl.when(z > 0)
            def _():
                wave_copy(k).start()

            mid = (taken + delta_mid[k]).astype(BF16)
            middle[k] = mid
            grad_ref[:, columns(side, k)] = jnp.where(side == 1, mid, low)
            other[k] = jnp.where(side == 1, low, mid)
            grad_copy(k).start()

        if k < lag:
            continue
        if k == lag:
            remote(mixed.at[side], mixed.at[away], mixed_s, mixed_r, partner).wait_recv()

        done = k - lag
        if done < n_chip:

            @pl.when(z < n_z - 1)
            def _():
                value_send((done + 1) % n_chip)

        out_parts[0, pl.ds(done * chunk, chunk)] = dot_rows(middle[done], mixed[0]).astype(BF16)
        out_parts[1, pl.ds(done * chunk, chunk)] = dot_rows(above[done], mixed[1]).astype(BF16)
        while sent < ready[0]:
            out_send(sent)
            sent += 1
        while (shared + 1) * rows <= (done + 1) * chunk:
            out_share(shared)
            shared += 1
        ready = ready[1:] + [shared]
    while sent < shared:
        out_send(sent)
        sent += 1

    @pl.when(z == n_z - 1)
    def _():
        value_gradient()
        for step in range(n_chip):
            value_send(step)

    total = value_pre[chip].astype(F32)
    for step in range(1, n_chip):
        source = peer(step) // 2
        remote(value_pre.at[0], value_in.at[source], vsum_s.at[step], vsum_r.at[source], sibling).wait_recv()
        total = total + value_in[source].astype(F32)
    sum_value_ref[...] = total

    total = jnp.zeros((rows, head), F32)
    for source in range(n_chip):
        @pl.when((my_half != side) | (source != chip))
        def _():
            remote(out_pre.at[0], out_in.at[source], osum_s.at[0], osum_r.at[source], sibling).wait_recv()

        total = total + out_in[source].astype(F32)
    sum_out_ref[...] = total

    for k in range(chunk_count):
        grad_copy(k).wait_send()
        remote(other.at[k], grad_ref.at[:, columns(away, k)], grad_s.at[k], grad_r.at[k], partner).wait_recv()

    pair_copy.wait_send()
    turned_copy.wait_send()
    head_copy.wait_send()
    backs_copy.wait_send()
    mixed_copy.wait_send()
    each_step(0, lambda step: outw_copy(step).wait_send())
    each_step(1, lambda step: outw_on(step).wait_send())
    value_spot(me, lambda spot: each_step(0, lambda step: value_copy(step, spot).wait_send()))
    each_step(1, lambda step: value_spot(peer(step), lambda spot: value_on(step, spot).wait_send()))

    @pl.when(my_half == away)
    def _():
        each_step(0, lambda step: near_copy(step).wait_send())

    for i in range(half_dp // 2):
        near_on(i, core).wait_send()
    each_step(0, lambda i: vcore_copy(i).wait_send())
    each_step(1, lambda step: vsum_copy(step).wait_send())
    each_cross_on(lambda slot, target: cross_on(slot, target).wait_send())

    def part_sent(slot, carry):
        @pl.when((slot != my_slot) & used(slot, side))
        def _():
            part_copy(slot).wait_send()

        return carry

    lax.fori_loop(z, n_z, part_sent, 0)

    @pl.when(sums_here)
    def _():
        for target in (0, 1):
            each_step(0, lambda step: cross_copy(step, target).wait_send())

    for layer in (0, 1):
        for i in range(half_dp):
            @pl.when(i % 2 != core)
            def _():
                ocore_copy(layer, i).wait_send()

            @pl.when((i % 2 == core) & jnp.logical_not(is_own(layer, i)))
            def _():
                osum_copy(layer, i).wait_send()

    @pl.when(z > reach)
    def _():
        for copy in top_copies():
            copy.wait_send()

    def gather_sent(k, carry):
        slot, here, onward = climbing(k)

        @pl.when(goes_down(k))
        def _():
            for copy in layer_copies(z + k, layer_rows.at[z + k]):
                copy.wait_send()

        @pl.when(onward)
        def _():
            for copy in climb_copies(slot, layer_rows.at[slot]):
                copy.wait_send()

        return carry

    lax.fori_loop(1, reach + 1, gather_sent, 0)

    @pl.when(z > 0)
    def _():
        for copy in layer_copies(z, value_ref):
            copy.wait_send()
        for k in range(chunk_count):
            wave_copy(k).wait_send()

    @pl.when(z > 0)
    def _():
        def line_sent(slot, carry):
            line_copy(slot).wait_send()
            return carry

        lax.fori_loop(z, n_z, line_sent, 0)


def shards(acts, scores, segments, cotangent, w_value, w_out):
    n_dp = lax.axis_size("dp")
    n_z = lax.axis_size("section") // 2
    tokens = acts[0]
    row_count, feat_width = tokens.shape
    seq_len = segments.shape[1]
    shard_rows, head = w_value.shape[1:]
    half = feat_width // 2
    chunk = 256 if half % 256 == 0 else 128
    chunks = half // chunk

    vmem = pl.BlockSpec(memory_space=pltpu.VMEM)
    dma = pltpu.SemaphoreType.DMA
    one, per_z, per_dp, per_chunk, per_chip = dma, dma((n_z,)), dma((n_dp,)), dma((chunks,)), dma((n_dp // 2,))
    grad_input, grad_value, grad_out = pl.pallas_call(
        functools.partial(kernel, n_z, n_dp, chunk),
        out_shape=(
            jax.ShapeDtypeStruct((row_count, feat_width), BF16),
            jax.ShapeDtypeStruct((shard_rows, head), F32),
            jax.ShapeDtypeStruct((shard_rows, head), F32),
        ),
        in_specs=[vmem] * 7,
        out_specs=(vmem,) * 3,
        scratch_shapes=[
            pltpu.VMEM((2, seq_len, 128), BF16),
            pltpu.VMEM((feat_width, head), BF16),
            pltpu.VMEM((half, 2 * head), BF16),
            pltpu.VMEM((half, head), BF16),
            pltpu.VMEM((shard_rows, 2 * head), BF16),
            pltpu.VMEM((n_z, shard_rows, head), BF16),
            pltpu.VMEM((n_z, head, 2 * head), BF16),
            pltpu.VMEM((n_dp, head, 2 * head), BF16),
            pltpu.VMEM((n_z, 2 * head, 2 * head), BF16),
            pltpu.VMEM((seq_len, 2 * head), F32),
            pltpu.VMEM((seq_len, head), F32),
            pltpu.VMEM((2 * head, 3 * head), BF16),
            pltpu.VMEM((seq_len, 3 * head), F32),
            pltpu.VMEM((2, seq_len, 128), BF16),
            pltpu.VMEM((n_z, seq_len, 2 * head), BF16),
            pltpu.VMEM((row_count, 2 * head), BF16),
            pltpu.VMEM((2, row_count, head), BF16),
            pltpu.VMEM((chunks, row_count, chunk), F32),
            pltpu.VMEM((chunks, row_count, chunk), F32),
            pltpu.VMEM((chunks, row_count, chunk), BF16),
            pltpu.VMEM((chunks, row_count, chunk), BF16),
            pltpu.VMEM((chunks, row_count, chunk), BF16),
            pltpu.VMEM((chunks, row_count, chunk), BF16),
            pltpu.VMEM((2, half, head), BF16),
            pltpu.VMEM((feat_width, head), BF16),
            pltpu.VMEM((n_dp // 2, shard_rows, head), BF16),
            pltpu.VMEM((n_dp // 2, shard_rows, head), BF16),
            pltpu.VMEM((n_dp // 2, shard_rows, head), BF16),
            pltpu.VMEM((n_dp // 2, shard_rows, head), BF16),
            pltpu.VMEM((n_dp // 2, shard_rows, head), BF16),
            pltpu.VMEM((n_dp // 2, shard_rows, head), BF16),
            *([one] * 10),
            dma((2 * n_z,)),
            dma((2 * n_z,)),
            dma((2 * n_z,)),
            per_chip,
            per_dp,
            per_chip,
            per_chip,
            per_dp,
            per_chip,
            per_chip,
            per_chip,
            per_chip,
            per_z,
            per_dp,
            per_dp,
            dma((2 * n_z,)),
            dma((2 * n_z,)),
            per_z,
            per_z,
            per_chunk,
            per_chunk,
            per_chunk,
            per_chunk,
            per_chip,
            per_chip,
            per_chip,
            per_chip,
            per_chip,
            per_chip,
            per_chip,
            per_chip,
        ],
        compiler_params=pltpu.CompilerParams(
            collective_id=0, has_side_effects=True, vmem_limit_bytes=52 << 20
        ),
        name="backward",
    )(tokens, cotangent, scores[0], segments[:, None, :], segments[:, :, None], w_value[0], w_out[0])
    return (grad_input[None], grad_value[None], grad_out[None])


def solution(mesh):
    placed = (
        P("section", "dp", None),
        P("section", "dp", None, None),
        P("dp", None),
        P("dp", None),
        P("section", "dp", None),
        P("section", "dp", None),
    )
    return jax.shard_map(
        shards,
        mesh=mesh,
        in_specs=placed,
        out_specs=(P("section", "dp", None), P("section", "dp", None), P("section", "dp", None)),
        check_vma=False,
    )
```
